256 devices in a mesh: row: 16 (over x, z_hi, core), col: 16 (over z_lo, y).
Axes of the slice: x: 4, y: 4, z: 8 (z_hi: 2, z_lo: 4; z = z_hi * 4 + z_lo), core: 2. Of those that a mesh axis runs over, the one named last changes fastest.
Arguments:
- latent: bfloat16 [256, 256, 512], P('row', 'col'), may hold values from -6 to 6
- grad_latent: bfloat16 [256, 256, 512], P('row', 'col'), may hold values from -6 to 6
- w_qkv_row: bfloat16 [512, 1536], replicated, may hold values from -0.25 to 0.25
- w_out_row: bfloat16 [512, 512], replicated, may hold values from -0.25 to 0.25
- w_qkv_col: bfloat16 [512, 1536], replicated, may hold values from -0.25 to 0.25
- w_out_col: bfloat16 [512, 512], replicated, may hold values from -0.25 to 0.25
Outputs:
- final: bfloat16 [256, 256, 512], P('row', 'col')
- grad_input: bfloat16 [256, 256, 512], P('row', 'col')
- grad_qkv_row: float32 [512, 1536], P('row', 'col')
- grad_out_row: float32 [512, 512], P('row', 'col')
- grad_qkv_col: float32 [512, 1536], P('row', 'col')
- grad_out_col: float32 [512, 512], P('row', 'col')
The draws below stay inside these ranges and needn't reach their ends.
All inputs are finite; a program needn't handle non-finite values.
Results may differ from the reference program's by a relative error of at most 0.04.
Values may be sent and summed in bfloat16 or wider, within the bound.
No kernel may reach another device: no remote copies, remote signals or barrier semaphores. Data moves between devices by JAX's collectives and lax.ppermute only.
A program may use at most 128 MiB of HBM per device.

```python
import math
import jax
import jax.numpy as jnp
from jax import lax

D = 512
HEADS = 8
HD = 64
NR = 256
NC = 256


def spiked(values, key, source, target, blocks, factor):
    def block_of(dim):
        return (jnp.arange(values.shape[dim]) // (values.shape[dim] // blocks)).reshape((-1,) + (1,) * (values.ndim - 1 - dim))

    one_side = jax.random.permutation(key, blocks)[block_of(target)]
    other_side = (block_of(target) + blocks // 2) % blocks
    return jnp.where((block_of(source) == one_side) | (block_of(source) == other_side), factor * values, values)


def levels(stream_key, dims, cuts, least, top_value):
    gain = 1.0
    for dim, blocks in cuts:
        heights = jax.random.uniform(jax.random.fold_in(jax.random.fold_in(stream_key, 6), dim), (blocks,), jnp.float32, least / len(cuts), top_value / len(cuts))
        gain = gain * jnp.repeat(jnp.exp(heights), dims[dim] // blocks).reshape((-1,) + (1,) * (len(dims) - 1 - dim))
    return gain


def scatter_about(key, shape, spread, bound, shards=(), dtype=jnp.bfloat16):
    level = levels(key, shape, shards, -0.22, 0.18) if shards else 1.0
    array = jax.random.normal(key, shape, jnp.float32) * spread * level
    return jnp.minimum(jnp.maximum(array, -bound), bound).astype(dtype)


def heavy_noise(own_key, shape, deviation, bound, pieces, heavy, kind=jnp.bfloat16):
    array = deviation * jax.random.normal(own_key, shape, jnp.float32)
    if pieces:
        array = array * levels(own_key, shape, pieces, -0.22, 0.18)
    return jnp.clip(spiked(array, jax.random.fold_in(own_key, 3), *heavy), -bound, bound).astype(kind)


def setup_inputs(seed: int = 0) -> dict:
    arg_keys = jax.random.split(jax.random.key(seed), 7)
    return {
        "latent": scatter_about(arg_keys[0], (NR, NC, D), 1.0, 6.0, ((0, 16), (1, 16))),
        "grad_latent": heavy_noise(arg_keys[1], (NR, NC, D), 1.0, 6.0, ((0, 16), (1, 16)), (0, 2, 16, 2.0)),
        "w_qkv_row": scatter_about(arg_keys[2], (D, 3 * D), D ** -0.5, 0.25),
        "w_out_row": scatter_about(arg_keys[3], (D, D), D ** -0.5, 0.25),
        "w_qkv_col": scatter_about(arg_keys[4], (D, 3 * D), D ** -0.5, 0.25),
        "w_out_col": scatter_about(arg_keys[5], (D, D), D ** -0.5, 0.25),
    }


EPS = 1e-06

def rms_rows(values):
    return values * lax.rsqrt(lax.optimization_barrier(jnp.mean(values * values, axis=-1, keepdims=True)) + EPS)

def head_norm(qkv):
    parts = qkv.reshape(qkv.shape[:-1] + (3, HEADS, HD))
    scale = lax.rsqrt(lax.optimization_barrier(jnp.mean(parts * parts, axis=-1, keepdims=True)) + EPS)
    keep = (jnp.arange(3) == 2)[:, None, None]
    normed = jnp.where(keep, parts, parts * scale)
    return normed.reshape(qkv.shape)

def attention(qkvn, form):
    lead = qkvn.shape[:-1]
    parts = qkvn.astype(jnp.float32).reshape(lead + (3, HEADS, HD))
    query = parts[..., 0, :, :]
    keys = parts[..., 1, :, :]
    values = parts[..., 2, :, :]
    if form == 'row':
        scores = jnp.einsum('bqhe,bkhe->bhqk', query, keys) / math.sqrt(HD)
    else:
        scores = jnp.einsum('qbhe,kbhe->bhqk', query, keys) / math.sqrt(HD)
    expo = jnp.exp(scores)
    weights = expo / lax.optimization_barrier(jnp.sum(expo, axis=-1, keepdims=True))
    rounded = lax.optimization_barrier(weights.astype(jnp.bfloat16)).astype(jnp.float32)
    if form == 'row':
        mixed = jnp.einsum('bhqk,bkhe->bqhe', rounded, values)
    else:
        mixed = jnp.einsum('bhqk,kbhe->qbhe', rounded, values)
    return mixed.reshape(lead + (HEADS * HD,))

def along_lines(qkvn, across):
    lines = jnp.swapaxes(qkvn, 0, 1) if across else qkvn
    result = lax.map(lambda line: attention(line[None], 'row')[0].astype(jnp.bfloat16), lines)
    return jnp.swapaxes(result, 0, 1) if across else result

def pull_lines(qkvn, grad_mixed, across):
    lines = jnp.swapaxes(qkvn, 0, 1) if across else qkvn
    grads = jnp.swapaxes(grad_mixed, 0, 1) if across else grad_mixed

    def one_line(pair):
        line, grad_line = pair
        _, pull = jax.vjp(lambda a: attention(a[None], 'row')[0], line)
        return pull(grad_line.astype(jnp.float32))[0].astype(jnp.bfloat16)
    result = lax.map(one_line, (lines, grads))
    return jnp.swapaxes(result, 0, 1) if across else result

def forward(latent_in, w_qkv, w_out, across):
    normed = rms_rows(latent_in.astype(jnp.float32)).astype(jnp.bfloat16)
    qkv = jnp.dot(normed, w_qkv, preferred_element_type=jnp.float32)
    qkvn = head_norm(qkv).astype(jnp.bfloat16)
    mixed = along_lines(qkvn, across)
    result = latent_in.astype(jnp.float32) + jnp.dot(mixed, w_out, preferred_element_type=jnp.float32)
    return (result.astype(jnp.bfloat16), (normed, qkv, qkvn, mixed))

def backward(latent_in, grad_out, w_qkv, w_out, saved, across):
    normed, qkv, qkvn, mixed = saved
    grad_w_out = jnp.einsum('abd,abe->de', mixed.astype(jnp.float32), grad_out.astype(jnp.float32))
    grad_mixed = jnp.einsum('abe,de->abd', grad_out.astype(jnp.float32), w_out.astype(jnp.float32)).astype(jnp.bfloat16)
    grad_qkvn = pull_lines(qkvn, grad_mixed, across)
    _, pull_norm = jax.vjp(head_norm, qkv)
    grad_qkv = pull_norm(grad_qkvn.astype(jnp.float32))[0].astype(jnp.bfloat16)
    grad_w_qkv = jnp.einsum('abd,abe->de', normed.astype(jnp.float32), grad_qkv.astype(jnp.float32))
    grad_normed = jnp.einsum('abe,de->abd', grad_qkv.astype(jnp.float32), w_qkv.astype(jnp.float32)).astype(jnp.bfloat16)
    _, pull_rms = jax.vjp(rms_rows, latent_in.astype(jnp.float32))
    grad_x = grad_out.astype(jnp.float32) + pull_rms(grad_normed.astype(jnp.float32))[0]
    return (grad_x.astype(jnp.bfloat16), grad_w_qkv, grad_w_out)

def reference(latent, grad_latent, w_qkv_row, w_out_row, w_qkv_col, w_out_col):
    middle, saved_row = forward(latent, w_qkv_row, w_out_row, False)
    final, saved_col = forward(middle, w_qkv_col, w_out_col, True)
    grad_middle, grad_qkv_col, grad_out_col = backward(middle, grad_latent, w_qkv_col, w_out_col, saved_col, True)
    grad_input, grad_qkv_row, grad_out_row = backward(latent, grad_middle, w_qkv_row, w_out_row, saved_row, False)
    return (final, grad_input, grad_qkv_row, grad_out_row, grad_qkv_col, grad_out_col)
```

```python
import functools

import jax
import jax.numpy as jnp
from jax import lax
from jax.experimental import pallas as pl
from jax.experimental.pallas import tpu as pltpu
from jax.sharding import Mesh
from jax.sharding import PartitionSpec as P

HEADS = 8
HD = 64
CH = 512
EPS = 1e-06
F32 = jnp.float32
BF16 = jnp.bfloat16

ROW = ("x", "zh", "core")
COL = ("zl", "y")
CHIP = ("zl", "y", "x", "zh")


def nn(a, b):
    return jnp.dot(a, b, preferred_element_type=F32)


def nt(a, b):
    return lax.dot_general(a, b, (((1,), (1,)), ((), ())), preferred_element_type=F32)


def tn(a, b):
    return lax.dot_general(a, b, (((0,), (0,)), ((), ())), preferred_element_type=F32)


def split2(a):
    hi = a.astype(BF16)
    return hi, (a - hi.astype(F32)).astype(BF16)


def iota(shape, dim):
    return lax.broadcasted_iota(jnp.int32, shape, dim)


def head_map():
    shape = (2 * CH, 128)
    return (iota(shape, 0) // HD == iota(shape, 1)).astype(BF16)


def head_mean(values, heads):
    hi, lo = split2(values)
    return (nn(hi, heads) + nn(lo, heads)) * (1.0 / HD)


def head_spread(values, heads):
    hi, lo = split2(values)
    return nt(hi, heads) + nt(lo, heads)


def inv_rms(x):
    return lax.rsqrt(jnp.mean(x * x, axis=-1, keepdims=True) + EPS)


def swap_order(values):
    rows = iota((256, 256), 0)
    cols = iota((256, 256), 1)
    swap = ((rows & 15) * 16 + (rows >> 4) == cols).astype(BF16)
    return nn(swap, values).astype(BF16)


def project(x, w_qkv, heads):
    normed = (x * inv_rms(x)).astype(BF16)
    qkv = nn(normed, w_qkv)
    qk = qkv[:, : 2 * CH]
    scale = lax.rsqrt(head_mean(qk * qk, heads) + EPS)
    qkn = (qk * head_spread(scale, heads)).astype(BF16)
    return normed, scale, qkn, qkv[:, 2 * CH :].astype(BF16)


def low_half():
    return iota((256, 128), 1) < HD


def only(half, values):
    low = low_half()
    keep = low if half == 0 else jnp.logical_not(low)
    return jnp.where(keep, values, jnp.zeros_like(values))


def softmax(query, keys):
    expo = jnp.exp(nt(query, keys) * 0.125)
    return expo * (1.0 / jnp.sum(expo, axis=-1, keepdims=True))


def attend(qkn, v, pair):
    at = slice(pair * 128, pair * 128 + 128)
    q2, k2, v2 = qkn[:, at], qkn[:, CH + pair * 128 : CH + pair * 128 + 128], v[:, at]
    parts = [nn(softmax(only(h, q2), k2).astype(BF16), v2) for h in range(2)]
    return jnp.where(low_half(), parts[0], parts[1])


def attend_back(qkn, v, gmix, gmix_t, q_t, pair, mixed=None):
    at = slice(pair * 128, pair * 128 + 128)
    q2, k2, v2 = qkn[:, at], qkn[:, CH + pair * 128 : CH + pair * 128 + 128], v[:, at]
    g2 = gmix[:, at]
    g2f = g2.astype(F32)
    low = low_half()
    mix, gq, gk, gv = [], [], [], []
    for h in range(2):
        rows = slice(pair * 128 + h * HD, pair * 128 + h * HD + HD)
        weights = softmax(only(h, q2), k2)
        rounded = weights.astype(BF16)
        mix.append(nn(rounded, v2))
        gweights = nt(only(h, g2), v2)
        inner = jnp.sum(only(h, g2f * mix[h]), axis=-1, keepdims=True)
        gscores = (weights * (gweights - inner) * 0.125).astype(BF16)
        gv.append(nn(gmix_t[rows], rounded))
        gq.append(nn(gscores, k2))
        gk.append(nn(q_t[rows], gscores))
    return (
        jnp.where(low, mix[0], mix[1]),
        jnp.where(low, gq[0], gq[1]),
        jnp.concatenate(gk, axis=0),
        jnp.concatenate(gv, axis=0),
    )


def forward_kernel(x_ref, wq_ref, wo_ref, mid_ref, normed_ref, scale_ref, qkn_ref, v_ref, mixed_ref):
    x = x_ref[...].astype(F32)
    heads = head_map()
    normed, scale, qkn, v = project(x, wq_ref[...], heads)
    normed_ref[...] = normed
    scale_ref[...] = scale
    qkn_ref[...] = qkn
    v_ref[...] = v
    for pair in range(HEADS // 2):
        mixed_ref[:, pair * 128 : pair * 128 + 128] = attend(qkn, v, pair).astype(BF16)
    y = (x + nn(mixed_ref[...], wo_ref[...])).astype(BF16)
    mid_ref[...] = swap_order(y)


def backward_tail(x, g, wq_ref, scale, qkn, v, gmix, gmix_t, heads, mixed_ref, gqkv_ref, gx_ref):
    q_t = qkn[:, :CH].T
    gqs, gks, gvs = [], [], []
    for pair in range(HEADS // 2):
        mix, gq, gk, gv = attend_back(qkn, v, gmix, gmix_t, q_t, pair)
        if mixed_ref is not None:
            mixed_ref[:, pair * 128 : pair * 128 + 128] = mix.astype(BF16)
        gqs.append(gq.astype(BF16))
        gks.append(gk.astype(BF16).T)
        gvs.append(gv.astype(BF16).T)
    gqk = jnp.concatenate(gqs + gks, axis=1).astype(F32)
    yn = qkn.astype(F32)
    inner = head_spread(head_mean(yn * gqk, heads), heads)
    gqk = head_spread(scale, heads) * (gqk - yn * inner)
    gqkv_ref[:, : 2 * CH] = gqk.astype(BF16)
    gqkv_ref[:, 2 * CH :] = jnp.concatenate(gvs, axis=1)
    gnormed = nt(gqkv_ref[...], wq_ref[...]).astype(BF16).astype(F32)
    r = inv_rms(x)
    xn = x * r
    gx = g + r * (gnormed - xn * jnp.mean(xn * gnormed, axis=-1, keepdims=True))
    gx_ref[...] = gx.astype(BF16)


def both_kernel(x_ref, g_ref, wq_ref, wo_ref, y_ref, gx_ref, normed_ref, mixed_ref, gqkv_ref):
    x = x_ref[...].astype(F32)
    heads = head_map()
    normed, scale, qkn, v = project(x, wq_ref[...], heads)
    normed_ref[...] = normed
    g = g_ref[...]
    gmix = nt(g, wo_ref[...]).astype(BF16)
    gmix_t = nt(wo_ref[...], g).astype(BF16)
    backward_tail(
        x, g.astype(F32), wq_ref, scale, qkn, v, gmix, gmix_t, heads, mixed_ref, gqkv_ref, gx_ref
    )
    y_ref[...] = (x + nn(mixed_ref[...], wo_ref[...])).astype(BF16)


def back_kernel(x_ref, g_ref, wq_ref, wo_ref, scale_ref, qkn_ref, v_ref, gx_ref, gqkv_ref, gs_ref):
    g = swap_order(g_ref[...])
    gs_ref[...] = g
    gmix = nt(g, wo_ref[...]).astype(BF16)
    gmix_t = nt(wo_ref[...], g).astype(BF16)
    backward_tail(
        x_ref[...].astype(F32),
        g.astype(F32),
        wq_ref,
        scale_ref[...],
        qkn_ref[...],
        v_ref[...],
        gmix,
        gmix_t,
        head_map(),
        None,
        gqkv_ref,
        gx_ref,
    )


def weights_kernel(place, core_ref, normed_ref, mixed_ref, gqkv_ref, g_ref, keep_ref, send_ref):
    core = core_ref[0]
    row = iota((CH, CH), 0)
    col = iota((CH, CH), 1)
    bit = (col >> 8) ^ core
    order = (row == ((col >> 5) & 7) * 64 + bit * 32 + (col & 31)).astype(BF16)
    normed = nn(normed_ref[...], order).astype(BF16)
    mixed = nn(mixed_ref[...], order).astype(BF16)
    col3 = iota((384, CH), 1)
    lane3 = col3 & 127
    spread3 = ((iota((384, CH), 0) == (col3 >> 7) * 96 + lane3) & (lane3 < 96)).astype(BF16)
    col1 = iota((128, CH), 1)
    lane1 = col1 & 127
    spread1 = ((iota((128, CH), 0) == (col1 >> 7) * 32 + lane1 - 96) & (lane1 >= 96)).astype(BF16)
    for group in range(4):
        gq = nn(gqkv_ref[:, group * 384 : group * 384 + 384], spread3).astype(BF16)
        gg = nn(g_ref[:, group * 128 : group * 128 + 128], spread1).astype(BF16)
        total = (tn(normed, gq) + tn(mixed, gg)).astype(BF16)
        for slot, ref in ((0, keep_ref), (1, send_ref)):
            for xz in range(8):
                rows = slice(slot * 256 + xz * 32, slot * 256 + xz * 32 + 32)
                for y in range(4):
                    ref[place(group, y, xz >> 1, xz & 1)] = total[rows, y * 128 : y * 128 + 128]


VMEM = pl.BlockSpec(memory_space=pltpu.VMEM)
SMEM = pl.BlockSpec(memory_space=pltpu.SMEM)


def shape(rows, cols, dtype=BF16):
    return jax.ShapeDtypeStruct((rows, cols), dtype)


def call(kernel, outs, specs, flops, args):
    nbytes = sum(a.size * a.dtype.itemsize for a in (*args, *outs))
    return pl.pallas_call(
        kernel,
        out_shape=outs,
        in_specs=specs,
        out_specs=[VMEM] * len(outs),
        compiler_params=pltpu.CompilerParams(vmem_limit_bytes=48 * 2**20),
        cost_estimate=pl.CostEstimate(flops=flops, bytes_accessed=nbytes, transcendentals=2**19),
    )(*args)


def weight_terms(place, core, normed, mixed, gqkv, g):
    outs = [jax.ShapeDtypeStruct((128, 32, 128), BF16)] * 2
    return call(
        functools.partial(weights_kernel, place),
        outs,
        [SMEM] + [VMEM] * 4,
        2 * 10**9,
        (core, normed, mixed, gqkv, g),
    )


def swap_cores(values):
    return lax.ppermute(values, "core", [(0, 1), (1, 0)])


def a2a(values, axes):
    return lax.all_to_all(values, axes, split_axis=0, concat_axis=0, tiled=True)


def add(a, b):
    return (a.astype(F32) + b.astype(F32)).astype(BF16)


def chip_place(zl, y, x, zh):
    return ((zl * 4 + y) * 4 + x) * 2 + zh


def ring_place(zl, y, x, zh):
    return ((y * 4 + x) * 2 + zh) * 4 + zl


def on_device(latent, grad_latent, w_qkv_row, w_out_row, w_qkv_col, w_out_col):
    core = lax.axis_index("core").astype(jnp.int32).reshape(1)
    x_row = a2a(latent, COL).reshape(256, CH)
    g_col = a2a(jnp.swapaxes(grad_latent, 0, 1), ROW).reshape(256, CH)
    mid_row, normed_r, scale_r, qkn_r, v_r, mixed_r = call(
        forward_kernel,
        [
            shape(256, CH),
            shape(256, CH),
            shape(256, 128, F32),
            shape(256, 2 * CH),
            shape(256, CH),
            shape(256, CH),
        ],
        [VMEM] * 3,
        10**9,
        (x_row, w_qkv_row, w_out_row),
    )
    x_col = a2a(mid_row, ROW + COL)
    y_col, gx_col, normed_c, mixed_c, gqkv_c = call(
        both_kernel,
        [shape(256, CH)] * 4 + [shape(256, 3 * CH)],
        [VMEM] * 4,
        3 * 10**9,
        (x_col, g_col, w_qkv_col, w_out_col),
    )
    g_row = a2a(gx_col, ROW + COL)
    keep_c, send_c = weight_terms(ring_place, core, normed_c, mixed_c, gqkv_c, g_col)
    sum_c = add(keep_c, swap_cores(send_c)).reshape(4, 4, 8, 32, 128)
    sum_c = lax.psum_scatter(sum_c, "y", scatter_dimension=0, tiled=False)
    sum_c = lax.psum_scatter(sum_c, "x", scatter_dimension=0, tiled=False)
    sum_c = lax.psum_scatter(sum_c, ("zh", "zl"), scatter_dimension=0, tiled=False).astype(F32)
    final = jnp.swapaxes(a2a(y_col.reshape(16, 16, CH), ROW), 0, 1)
    gx_row, gqkv_r, gs_r = call(
        back_kernel,
        [shape(256, CH), shape(256, 3 * CH), shape(256, CH)],
        [VMEM] * 7,
        2 * 10**9,
        (x_row, g_row, w_qkv_row, w_out_row, scale_r, qkn_r, v_r),
    )
    grad_input = a2a(gx_row.reshape(16, 16, CH), COL)
    keep_r, send_r = weight_terms(chip_place, core, normed_r, mixed_r, gqkv_r, gs_r)
    sum_r = a2a(add(keep_r, swap_cores(send_r)), CHIP)
    sum_r = jnp.sum(sum_r.astype(F32), axis=0)
    return (final, grad_input, sum_r[:, :96], sum_r[:, 96:], sum_c[:, :96], sum_c[:, 96:])


def solution(mesh):
    fine = Mesh(mesh.devices.reshape(4, 2, 2, 4, 4), ("x", "zh", "core", "zl", "y"))
    in_specs = (P(ROW, COL, None), P(ROW, COL, None), P(), P(), P(), P())
    out_specs = (
        P(ROW, COL, None),
        P(ROW, COL, None),
        P(ROW, COL),
        P(ROW, COL),
        P(ROW, COL),
        P(ROW, COL),
    )
    return jax.shard_map(
        on_device, mesh=fine, in_specs=in_specs, out_specs=out_specs, check_vma=False
    )
```

```python
import jax
import jax.numpy as jnp
from jax import lax
from jax.experimental import pallas as pl
from jax.experimental.pallas import tpu as pltpu
from jax.sharding import Mesh
from jax.sharding import PartitionSpec as P

HEADS = 8
HD = 64
CH = 512
EPS = 1e-06
F32 = jnp.float32
BF16 = jnp.bfloat16

ROW = ("x", "zh", "core")
COL = ("zl", "y")


def nn(a, b):
    return jnp.dot(a, b, preferred_element_type=F32)


def nt(a, b):
    return lax.dot_general(a, b, (((1,), (1,)), ((), ())), preferred_element_type=F32)


def tn(a, b):
    return lax.dot_general(a, b, (((0,), (0,)), ((), ())), preferred_element_type=F32)


def split2(a):
    hi = a.astype(BF16)
    return hi, (a - hi.astype(F32)).astype(BF16)


def iota(shape, dim):
    return lax.broadcasted_iota(jnp.int32, shape, dim)


def head_map():
    shape = (2 * CH, 128)
    return (iota(shape, 0) // HD == iota(shape, 1)).astype(BF16)


def head_mean(values, heads):
    hi, lo = split2(values)
    return (nn(hi, heads) + nn(lo, heads)) * (1.0 / HD)


def head_spread(values, heads):
    hi, lo = split2(values)
    return nt(hi, heads) + nt(lo, heads)


def inv_rms(x):
    return lax.rsqrt(jnp.mean(x * x, axis=-1, keepdims=True) + EPS)


def swap_order(values):
    rows = iota((256, 256), 0)
    cols = iota((256, 256), 1)
    swap = ((rows & 15) * 16 + (rows >> 4) == cols).astype(BF16)
    return nn(swap, values).astype(BF16)


def rows_from(source, values):
    return nn((iota((256, 256), 1) == source).astype(BF16), values).astype(BF16)


def absolute(at_ref, dx, zc, sign):
    my_x, my_zh, my_core = at_ref[0], at_ref[1], at_ref[2]
    return ((my_x + sign * dx) & 3) * 4 + (zc ^ (my_zh * 2 + my_core))


def pack_rows(at_ref, values, inner_first, refs):
    k = iota((256, 256), 0)
    device = absolute(at_ref, (k >> 4) & 3, k >> 6, 1)
    cell = k & 15
    source = device * 16 + cell if inner_first else cell * 16 + device
    packed = rows_from(source, values)
    for zc in range(4):
        refs[zc][...] = packed[zc * 64 : zc * 64 + 64]


def unpack_rows(at_ref, refs, cell_first):
    k = iota((256, 256), 0)
    device = (k & 15) if cell_first else (k >> 4)
    cell = (k >> 4) if cell_first else (k & 15)
    dx = (at_ref[0] - (device >> 2)) & 3
    zc = (device & 3) ^ (at_ref[1] * 2 + at_ref[2])
    values = jnp.concatenate([ref[...] for ref in refs], axis=0)
    return rows_from(dx * 64 + zc * 16 + cell, values)


def pack_kernel(at_ref, g_ref, *refs):
    pack_rows(at_ref, g_ref[...], False, refs)


def unpack_kernel(at_ref, a_ref, b_ref, c_ref, d_ref, out_ref):
    out_ref[...] = unpack_rows(at_ref, (a_ref, b_ref, c_ref, d_ref), True)


def regroup_kernel(*refs):
    for dx in range(4):
        for zc in range(4):
            refs[4 + dx][zc * 16 : zc * 16 + 16] = refs[zc][dx * 16 : dx * 16 + 16]


def project(x, w_qkv, heads):
    normed = (x * inv_rms(x)).astype(BF16)
    qkv = nn(normed, w_qkv)
    qk = qkv[:, : 2 * CH]
    scale = lax.rsqrt(head_mean(qk * qk, heads) + EPS)
    qkn = (qk * head_spread(scale, heads)).astype(BF16)
    return normed, scale, qkn, qkv[:, 2 * CH :].astype(BF16)


def low_half():
    return iota((256, 128), 1) < HD


def only(half, values):
    low = low_half()
    keep = low if half == 0 else jnp.logical_not(low)
    return jnp.where(keep, values, jnp.zeros_like(values))


def softmax(query, keys):
    expo = jnp.exp(nt(query, keys) * 0.125)
    return expo * (1.0 / jnp.sum(expo, axis=-1, keepdims=True))


def attend(qkn, v, pair):
    at = slice(pair * 128, pair * 128 + 128)
    q2, k2, v2 = qkn[:, at], qkn[:, CH + pair * 128 : CH + pair * 128 + 128], v[:, at]
    parts = [nn(softmax(only(h, q2), k2).astype(BF16), v2) for h in range(2)]
    return jnp.where(low_half(), parts[0], parts[1])


def attend_back(qkn, v, gmix, gmix_t, q_t, pair, recalled):
    at = slice(pair * 128, pair * 128 + 128)
    q2, k2, v2 = qkn[:, at], qkn[:, CH + pair * 128 : CH + pair * 128 + 128], v[:, at]
    g2 = gmix[:, at]
    g2f = g2.astype(F32)
    low = low_half()
    mix, gq, gk, gv = [], [], [], []
    for h in range(2):
        rows = slice(pair * 128 + h * HD, pair * 128 + h * HD + HD)
        if recalled is None:
            weights = softmax(only(h, q2), k2)
            rounded = weights.astype(BF16)
            mix.append(nn(rounded, v2))
            inner = jnp.sum(only(h, g2f * mix[h]), axis=-1, keepdims=True)
        else:
            rounded = recalled[0][2 * pair + h]
            weights = rounded.astype(F32)
            inner = jnp.sum(only(h, g2f * recalled[1][:, at].astype(F32)), axis=-1, keepdims=True)
        gweights = nt(only(h, g2), v2)
        gscores = (weights * (gweights - inner) * 0.125).astype(BF16)
        gv.append(nn(gmix_t[rows], rounded))
        gq.append(nn(gscores, k2))
        gk.append(nn(q_t[rows], gscores))
    return (
        jnp.where(low, mix[0], mix[1]) if recalled is None else None,
        jnp.where(low, gq[0], gq[1]),
        jnp.concatenate(gk, axis=0),
        jnp.concatenate(gv, axis=0),
    )


def forward_kernel(x_ref, wq_ref, wo_ref, mid_ref):
    x = x_ref[...].astype(F32)
    _, _, qkn, v = project(x, wq_ref[...], head_map())
    mixed = [attend(qkn, v, pair).astype(BF16) for pair in range(HEADS // 2)]
    y = (x + nn(jnp.concatenate(mixed, axis=1), wo_ref[...])).astype(BF16)
    mid_ref[...] = swap_order(y)


def recall_kernel(
    x_ref, wq_ref, normed_ref, scale_ref, qkn_ref, v_ref, q_t_ref, mixed_ref, weights_ref
):
    normed, scale, qkn, v = project(x_ref[...].astype(F32), wq_ref[...], head_map())
    normed_ref[...] = normed
    scale_ref[...] = scale
    qkn_ref[...] = qkn
    v_ref[...] = v
    q_t_ref[...] = qkn[:, :CH].T
    for pair in range(HEADS // 2):
        at = slice(pair * 128, pair * 128 + 128)
        q2, k2, v2 = qkn[:, at], qkn[:, CH + pair * 128 : CH + pair * 128 + 128], v[:, at]
        parts = []
        for h in range(2):
            rounded = softmax(only(h, q2), k2).astype(BF16)
            weights_ref[2 * pair + h] = rounded
            parts.append(nn(rounded, v2))
        mixed_ref[:, at] = jnp.where(low_half(), parts[0], parts[1]).astype(BF16)


def backward_tail(
    x, g, wq_ref, scale, qkn, v, q_t, gmix, gmix_t, heads, recalled, mixed_ref, gqkv_ref, gx_ref
):
    gqs, gks, gvs = [], [], []
    for pair in range(HEADS // 2):
        mix, gq, gk, gv = attend_back(qkn, v, gmix, gmix_t, q_t, pair, recalled)
        if mixed_ref is not None:
            mixed_ref[:, pair * 128 : pair * 128 + 128] = mix.astype(BF16)
        gqs.append(gq.astype(BF16))
        gks.append(gk.astype(BF16).T)
        gvs.append(gv.astype(BF16).T)
    gqk = jnp.concatenate(gqs + gks, axis=1).astype(F32)
    yn = qkn.astype(F32)
    inner = head_spread(head_mean(yn * gqk, heads), heads)
    gqk = head_spread(scale, heads) * (gqk - yn * inner)
    gqkv_ref[:, : 2 * CH] = gqk.astype(BF16)
    gqkv_ref[:, 2 * CH :] = jnp.concatenate(gvs, axis=1)
    gnormed = nt(gqkv_ref[...], wq_ref[...]).astype(BF16).astype(F32)
    r = inv_rms(x)
    xn = x * r
    gx = g + r * (gnormed - xn * jnp.mean(xn * gnormed, axis=-1, keepdims=True))
    gx_ref[...] = gx.astype(BF16)


def both_kernel(
    at_ref, x_ref, g0_ref, g1_ref, g2_ref, g3_ref, wq_ref, wo_ref,
    y0_ref, y1_ref, y2_ref, y3_ref, g_ref, gx_ref, normed_ref, mixed_ref, gqkv_ref,
):
    x = x_ref[...].astype(F32)
    heads = head_map()
    normed, scale, qkn, v = project(x, wq_ref[...], heads)
    normed_ref[...] = normed
    g = unpack_rows(at_ref, (g0_ref, g1_ref, g2_ref, g3_ref), False)
    g_ref[...] = g
    gmix = nt(g, wo_ref[...]).astype(BF16)
    gmix_t = nt(wo_ref[...], g).astype(BF16)
    backward_tail(
        x,
        g.astype(F32),
        wq_ref,
        scale,
        qkn,
        v,
        qkn[:, :CH].T,
        gmix,
        gmix_t,
        heads,
        None,
        mixed_ref,
        gqkv_ref,
        gx_ref,
    )
    y = (x + nn(mixed_ref[...], wo_ref[...])).astype(BF16)
    pack_rows(at_ref, y, True, (y0_ref, y1_ref, y2_ref, y3_ref))


def back_kernel(
    x_ref, g_ref, wq_ref, wo_ref, scale_ref, qkn_ref, v_ref, q_t_ref, mixed_ref, weights_ref,
    gx_ref, gqkv_ref, gs_ref,
):
    g = swap_order(g_ref[...])
    gs_ref[...] = g
    backward_tail(
        x_ref[...].astype(F32),
        g.astype(F32),
        wq_ref,
        scale_ref[...],
        qkn_ref[...],
        v_ref[...],
        q_t_ref[...],
        nt(g, wo_ref[...]).astype(BF16),
        nt(wo_ref[...], g).astype(BF16),
        head_map(),
        (weights_ref, mixed_ref),
        None,
        gqkv_ref,
        gx_ref,
    )


def finish_kernel(sums_ref, *refs):
    totals = jnp.sum(sums_ref[...].astype(F32), axis=0)
    for k in range(2):
        refs[2 * k][...] = totals[k, :, :96]
        refs[2 * k + 1][...] = totals[k, :, 96:]


def weights_kernel(at_ref, normed_ref, mixed_ref, gqkv_ref, g_ref, keep_ref, send_ref):
    my_y, core = at_ref[3], at_ref[2]
    row = iota((CH, CH), 0)
    col = iota((CH, CH), 1)
    bit = (col >> 8) ^ core
    order = (row == ((col >> 5) & 7) * 64 + bit * 32 + (col & 31)).astype(BF16)
    normed = nn(normed_ref[...], order).astype(BF16)
    mixed = nn(mixed_ref[...], order).astype(BF16)
    col3 = iota((384, CH), 1)
    lane3 = col3 & 127
    spread3 = ((iota((384, CH), 0) == (col3 >> 7) * 96 + lane3) & (lane3 < 96)).astype(BF16)
    col1 = iota((128, CH), 1)
    lane1 = col1 & 127
    spread1 = ((iota((128, CH), 0) == (col1 >> 7) * 32 + lane1 - 96) & (lane1 >= 96)).astype(BF16)
    for group in range(4):
        gq = nn(gqkv_ref[:, group * 384 : group * 384 + 384], spread3).astype(BF16)
        gg = nn(g_ref[:, group * 128 : group * 128 + 128], spread1).astype(BF16)
        total = (tn(normed, gq) + tn(mixed, gg)).astype(BF16)
        for slot, ref in ((0, keep_ref), (1, send_ref)):
            for xz in range(8):
                rows = slice(slot * 256 + xz * 32, slot * 256 + xz * 32 + 32)
                for y in range(4):
                    ref[(y - my_y) & 3, xz * 4 + group] = total[rows, y * 128 : y * 128 + 128]


VMEM = pl.BlockSpec(memory_space=pltpu.VMEM)
SMEM = pl.BlockSpec(memory_space=pltpu.SMEM)


def shape(rows, cols, dtype=BF16):
    return jax.ShapeDtypeStruct((rows, cols), dtype)


def call(kernel, outs, specs, args, flops=1):
    nbytes = 1 if flops == 1 else sum(a.size * a.dtype.itemsize for a in (*args, *outs))
    return pl.pallas_call(
        kernel,
        out_shape=outs,
        in_specs=specs,
        out_specs=[VMEM] * len(outs),
        compiler_params=pltpu.CompilerParams(vmem_limit_bytes=24 * 2**20),
        cost_estimate=pl.CostEstimate(flops=flops, bytes_accessed=nbytes, transcendentals=0),
    )(*args)


def weight_terms(at, normed, mixed, gqkv, g):
    outs = [jax.ShapeDtypeStruct((4, 32, 32, 128), BF16)] * 2
    return call(weights_kernel, outs, [SMEM] + [VMEM] * 4, (at, normed, mixed, gqkv, g))


def swap_cores(values):
    return lax.ppermute(values, "core", [(0, 1), (1, 0)])


def a2a(values, axes):
    return lax.all_to_all(values, axes, split_axis=0, concat_axis=0, tiled=True)


def total(parts, dtype=BF16):
    return sum(p.astype(F32) for p in parts).astype(dtype)


def ring_sum(parts, axes, dtype=BF16):
    n = len(parts)
    moved = [
        lax.ppermute(parts[k], axes, [(i, (i + k) % n) for i in range(n)]) for k in range(1, n)
    ]
    return total([parts[0]] + moved, dtype)


def core_sum(keep, send):
    moved = swap_cores(send)
    return [total([keep[k], moved[k]]) for k in range(4)]


def first_hop(parts):
    axes = ("zh", "core")
    return [parts[0]] + [
        lax.ppermute(parts[zc], axes, [(i, i ^ zc) for i in range(4)]) for zc in range(1, 4)
    ]


def second_hop(parts):
    parts = call(regroup_kernel, [shape(64, CH)] * 4, [VMEM] * 4, parts)
    return [parts[0]] + [
        lax.ppermute(parts[k], "x", [(i, (i + k) % 4) for i in range(4)]) for k in range(1, 4)
    ]


def together(*values):
    return lax.optimization_barrier(values)


def on_device(latent, grad_latent, w_qkv_row, w_out_row, w_qkv_col, w_out_col):
    at = [lax.axis_index(name) for name in ("x", "zh", "core", "y")]
    at = jnp.stack(at).astype(jnp.int32)
    cells, wide = shape(256, CH), shape(256, 3 * CH)
    grad_latent = grad_latent.reshape(256, CH)
    g_col = call(pack_kernel, [shape(64, CH)] * 4, [SMEM, VMEM], (at, grad_latent))
    g_col = first_hop(g_col)
    x_row = a2a(latent, COL).reshape(256, CH)
    (mid_row,) = call(
        forward_kernel, [cells], [VMEM] * 3, (x_row, w_qkv_row, w_out_row), 10**9
    )
    mid_row, g_col = together(mid_row, g_col)
    g_col = second_hop(g_col)
    x_col = a2a(mid_row, ROW + COL)
    *y_col, g_col, gx_col, normed_c, mixed_c, gqkv_c = call(
        both_kernel,
        [shape(64, CH)] * 4 + [cells] * 4 + [wide],
        [SMEM] + [VMEM] * 7,
        (at, x_col, *g_col, w_qkv_col, w_out_col),
        3 * 10**9,
    )
    g_row = a2a(gx_col, ROW + COL)
    y_col = first_hop(y_col)
    sum_c = core_sum(*weight_terms(at, normed_c, mixed_c, gqkv_c, g_col))
    late_x, gx_col = together(x_row, gx_col)
    normed_r, scale_r, qkn_r, v_r, q_t_r, mixed_r, weights_r = call(
        recall_kernel,
        [
            cells,
            shape(256, 128, F32),
            shape(256, 2 * CH),
            cells,
            shape(CH, 256),
            cells,
            jax.ShapeDtypeStruct((HEADS, 256, 256), BF16),
        ],
        [VMEM] * 2,
        (late_x, w_qkv_row),
    )
    g_row, sum_c, qkn_r = together(g_row, sum_c, qkn_r)
    gx_row, gqkv_r, gs_r = call(
        back_kernel,
        [cells, wide, cells],
        [VMEM] * 10,
        (x_row, g_row, w_qkv_row, w_out_row, scale_r, qkn_r, v_r, q_t_r, mixed_r, weights_r),
        2 * 10**9,
    )
    sum_c = ring_sum(sum_c, "y")
    gx_row, sum_c, y_col = together(gx_row, sum_c, y_col)
    grad_input = a2a(gx_row.reshape(16, 16, CH), COL)
    sum_r = core_sum(*weight_terms(at, normed_r, mixed_r, gqkv_r, gs_r))
    y_col = second_hop(y_col)
    sum_r = ring_sum(sum_r, "y")
    grad_input, sum_r, y_col = together(grad_input, sum_r, y_col)
    sums = a2a(jnp.stack([sum_r, sum_c], axis=1), ("x", "zh", "zl"))
    (final,) = call(unpack_kernel, [cells], [SMEM] + [VMEM] * 4, (at, *y_col))
    final = final.reshape(16, 16, CH)
    gq, go = shape(32, 96, F32), shape(32, 32, F32)
    return (final, grad_input, *call(finish_kernel, [gq, go] * 2, [VMEM], (sums,)))


def solution(mesh):
    fine = Mesh(mesh.devices.reshape(4, 2, 2, 4, 4), ("x", "zh", "core", "zl", "y"))
    in_specs = (P(ROW, COL, None), P(ROW, COL, None), P(), P(), P(), P())
    out_specs = (
        P(ROW, COL, None),
        P(ROW, COL, None),
        P(ROW, COL),
        P(ROW, COL),
        P(ROW, COL),
        P(ROW, COL),
    )
    return jax.shard_map(
        on_device, mesh=fine, in_specs=in_specs, out_specs=out_specs, check_vma=False
    )
```

```python
import functools

import jax
import jax.numpy as jnp
from jax import lax
from jax.experimental import pallas as pl
from jax.experimental.pallas import tpu as pltpu
from jax.sharding import Mesh
from jax.sharding import PartitionSpec as P

HEADS = 8
HD = 64
CH = 512
EPS = 1e-06
F32 = jnp.float32
BF16 = jnp.bfloat16

ROW = ("x", "zh", "core")
COL = ("zl", "y")


def nn(a, b):
    return jnp.dot(a, b, preferred_element_type=F32)


def nt(a, b):
    return lax.dot_general(a, b, (((1,), (1,)), ((), ())), preferred_element_type=F32)


def tn(a, b):
    return lax.dot_general(a, b, (((0,), (0,)), ((), ())), preferred_element_type=F32)


def iota(shape, dim):
    return lax.broadcasted_iota(jnp.int32, shape, dim)


def head_map():
    shape = (2 * CH, 128)
    lane = iota(shape, 1)
    return ((iota(shape, 0) // HD == (lane & 15)) & (lane < 32)).astype(BF16)


def head_mean(values, heads):
    return nn(values.astype(BF16), heads) * (1.0 / HD)


def head_spread(values, heads):
    high = values.astype(BF16)
    rest = (values - high.astype(F32)).astype(BF16)
    lane = iota(values.shape, 1)
    return nt(jnp.where(lane < 16, high, rest), heads)


def inv_rms(x):
    return lax.rsqrt(jnp.mean(x * x, axis=-1, keepdims=True) + EPS)


def swap_order(values):
    rows = iota((256, 256), 0)
    cols = iota((256, 256), 1)
    swap = ((rows & 15) * 16 + (rows >> 4) == cols).astype(BF16)
    return nn(swap, values).astype(BF16)


def rows_from(source, values):
    return nn((iota((256, 256), 1) == source).astype(BF16), values).astype(BF16)


def pack_rows(values, device, inner_first):
    row = iota((256, 256), 0)
    to, cell = device(row >> 6, (row >> 4) & 3), row & 15
    packed = rows_from(to * 16 + cell if inner_first else cell * 16 + to, values)
    return [packed[k * 64 : k * 64 + 64] for k in range(4)]


def unpack_rows(refs, away, cell_first):
    row = iota((256, 256), 0)
    device, cell = (row & 15, row >> 4) if cell_first else (row >> 4, row & 15)
    one, two = away(device)
    values = jnp.concatenate([ref[...] for ref in refs], axis=0)
    return rows_from(two * 64 + one * 16 + cell, values)


def row_device(at_ref, one, two):
    return ((at_ref[0] + two) & 3) * 4 + (one ^ (at_ref[1] * 2 + at_ref[2]))


def row_away(at_ref, device):
    return (device & 3) ^ (at_ref[1] * 2 + at_ref[2]), (at_ref[0] - (device >> 2)) & 3


def col_device(at_ref, one, two):
    return ((at_ref[3] + one) & 3) * 4 + ((at_ref[4] + two) & 3)


def col_away(at_ref, device):
    return (at_ref[3] - (device >> 2)) & 3, (at_ref[4] - (device & 3)) & 3


def pack_kernel(at_ref, g_ref, *refs):
    parts = pack_rows(g_ref[...], functools.partial(row_device, at_ref), False)
    for ref, part in zip(refs, parts):
        ref[...] = part


def unpack_kernel(at_ref, *refs):
    refs[8][...] = unpack_rows(refs[:4], functools.partial(row_away, at_ref), True)
    refs[9][...] = unpack_rows(refs[4:8], functools.partial(col_away, at_ref), False)


def regroup_kernel(*refs):
    n = len(refs) // 2
    for first in range(0, n, 4):
        for two in range(4):
            for one in range(4):
                part = refs[first + one][two * 16 : two * 16 + 16]
                refs[n + first + two][one * 16 : one * 16 + 16] = part


def project(x, w_qkv, heads):
    normed = (x * inv_rms(x)).astype(BF16)
    qkv = nn(normed, w_qkv[...])
    qk = qkv[:, : 2 * CH]
    scale = lax.rsqrt(head_mean(qk * qk, heads) + EPS)
    qkn = (qk * head_spread(scale, heads)).astype(BF16)
    return normed, scale, qkn, qkv[:, 2 * CH :].astype(BF16)


def low_half():
    return iota((256, 128), 1) < HD


def only(half, values):
    low = low_half()
    keep = low if half == 0 else jnp.logical_not(low)
    return jnp.where(keep, values, jnp.zeros_like(values))


def softmax(query, keys):
    expo = jnp.exp(nt(query, keys) * 0.125)
    return expo * (1.0 / jnp.sum(expo, axis=-1, keepdims=True))


def attend(qkn, v, pair):
    at = slice(pair * 128, pair * 128 + 128)
    q2, k2, v2 = qkn[:, at], qkn[:, CH + pair * 128 : CH + pair * 128 + 128], v[:, at]
    parts = [nn(softmax(only(h, q2), k2).astype(BF16), v2) for h in range(2)]
    return jnp.where(low_half(), parts[0], parts[1])


def attend_back(qkn, v, gmix, gmix_t, q_t, pair, recalled):
    at = slice(pair * 128, pair * 128 + 128)
    q2, k2, v2 = qkn[:, at], qkn[:, CH + pair * 128 : CH + pair * 128 + 128], v[:, at]
    g2 = gmix[:, at]
    g2f = g2.astype(F32)
    low = low_half()
    mix, gq, gk, gv = [], [], [], []
    for h in range(2):
        rows = slice(pair * 128 + h * HD, pair * 128 + h * HD + HD)
        if recalled is None:
            weights = softmax(only(h, q2), k2)
            rounded = weights.astype(BF16)
            mix.append(nn(rounded, v2))
            inner = jnp.sum(only(h, g2f * mix[h]), axis=-1, keepdims=True)
        else:
            rounded = recalled[0][2 * pair + h]
            weights = rounded.astype(F32)
            inner = jnp.sum(only(h, g2f * recalled[1][:, at].astype(F32)), axis=-1, keepdims=True)
        gweights = nt(only(h, g2), v2)
        gscores = (weights * (gweights - inner) * 0.125).astype(BF16)
        gv.append(nn(gmix_t[rows], rounded))
        gq.append(nn(gscores, k2))
        gk.append(nn(q_t[rows], gscores))
    return (
        jnp.where(low, mix[0], mix[1]) if recalled is None else None,
        jnp.where(low, gq[0], gq[1]),
        jnp.concatenate(gk, axis=0),
        jnp.concatenate(gv, axis=0),
    )


def forward_kernel(take, give):
    x = take(0)[...].astype(F32)
    _, _, qkn, v = project(x, take(1), head_map())
    mixed = [attend(qkn, v, pair).astype(BF16) for pair in range(HEADS // 2)]
    y = (x + nn(jnp.concatenate(mixed, axis=1), take(2)[...])).astype(BF16)
    give(0, swap_order(y).reshape(256, 2, 256))


def recall_kernel(take, give):
    normed, scale, qkn, v = project(take(0)[...].astype(F32), take(1), head_map())
    give(1, scale)
    give(2, qkn)
    give(3, v)
    give(4, qkn[:, :CH].T)
    weights, mixed = [], []
    for pair in range(HEADS // 2):
        at = slice(pair * 128, pair * 128 + 128)
        q2, k2, v2 = qkn[:, at], qkn[:, CH + pair * 128 : CH + pair * 128 + 128], v[:, at]
        parts = []
        for h in range(2):
            rounded = softmax(only(h, q2), k2).astype(BF16)
            weights.append(rounded)
            parts.append(nn(rounded, v2))
        mixed.append(jnp.where(low_half(), parts[0], parts[1]).astype(BF16))
    give(0, normed)
    give(6, jnp.concatenate(mixed, axis=1))
    give(5, jnp.stack(weights))


def backward_tail(
    x, g, take_wq, scale, qkn, v, q_t, gmix, gmix_t, heads, recalled, give_terms
):
    gqs, gks, gvs, mixed = [], [], [], []
    for pair in range(HEADS // 2):
        mix, gq, gk, gv = attend_back(qkn, v, gmix, gmix_t, q_t, pair, recalled)
        if recalled is None:
            mixed.append(mix.astype(BF16))
        gqs.append(gq.astype(BF16))
        gks.append(gk.astype(BF16).T)
        gvs.append(gv.astype(BF16).T)
    gqk = jnp.concatenate(gqs + gks, axis=1).astype(F32)
    yn = qkn.astype(F32)
    inner = head_spread(head_mean(yn * gqk, heads), heads)
    gqk = head_spread(scale, heads) * (gqk - yn * inner)
    gqk = gqk.astype(BF16)
    gqkv = [gqk[:, :CH], gqk[:, CH:], jnp.concatenate(gvs, axis=1)]
    give_terms(mixed, gqkv)
    gnormed = nt(jnp.concatenate(gqkv, axis=1), take_wq()[...]).astype(BF16).astype(F32)
    r = inv_rms(x)
    xn = x * r
    gx = g + r * (gnormed - xn * jnp.mean(xn * gnormed, axis=-1, keepdims=True))
    return gx.astype(BF16), mixed


def both_kernel(at_ref, take, give):
    x = take(0)[...].astype(F32).reshape(256, CH)
    heads = head_map()
    normed, scale, qkn, v = project(x, take(1), heads)
    g = unpack_rows([take(3 + k) for k in range(4)], functools.partial(row_away, at_ref), False)
    give(5, normed)
    give(10, g)
    wo = take(2)[...]

    def give_terms(mixed, gqkv):
        give(6, jnp.concatenate(mixed, axis=1))
        for k, part in enumerate(gqkv):
            give(7 + k, part)

    gx, mixed = backward_tail(
        x,
        g.astype(F32),
        lambda: take(1),
        scale,
        qkn,
        v,
        qkn[:, :CH].T,
        nt(g, wo).astype(BF16),
        nt(wo, g).astype(BF16),
        heads,
        None,
        give_terms,
    )
    give(0, gx.reshape(256, 2, 256))
    y = (x + nn(jnp.concatenate(mixed, axis=1), wo)).astype(BF16)
    for k, part in enumerate(pack_rows(y, functools.partial(row_device, at_ref), True)):
        give(1 + k, part)


def back_kernel(at_ref, take, give):
    g = swap_order(take(0)[...].astype(F32).reshape(256, CH).astype(BF16))
    give(7, g)
    wo = take(1)[...]
    gmix, gmix_t = nt(g, wo).astype(BF16), nt(wo, g).astype(BF16)
    v, recalled, qkn, q_t = take(2)[...], (take(3), take(4)), take(5)[...], take(6)[...]
    scale, x = take(7)[...], take(8)[...].astype(F32)
    gx, _ = backward_tail(
        x,
        g.astype(F32),
        lambda: take(9),
        scale,
        qkn,
        v,
        q_t,
        gmix,
        gmix_t,
        head_map(),
        recalled,
        lambda _, gqkv: [give(4 + k, part) for k, part in enumerate(gqkv)],
    )
    for k, part in enumerate(pack_rows(gx, functools.partial(col_device, at_ref), True)):
        give(k, part)


def finish_kernel(sums_ref, *refs):
    totals = jnp.sum(sums_ref[...].astype(F32), axis=0)
    for k in range(2):
        refs[2 * k][...] = totals[k, :, :96]
        refs[2 * k + 1][...] = totals[k, :, 96:]


def weights_kernel(at_ref, *refs):
    own, other, (out_ref, made, sems) = refs[:6], refs[6:12], refs[12:]
    ggs = (own[2:], other[2:])
    core = at_ref[2]
    col = iota((CH, 256), 1)
    order = (iota((CH, 256), 0) == (col >> 5) * 64 + core * 32 + (col & 31)).astype(BF16)
    row, col = iota((CH, CH), 0), iota((CH, CH), 1)
    lane = col & 127
    near = (row == (col >> 7) * 96 + lane) & (lane < 96)
    far = (row == 384 + (col >> 7) * 32 + lane - 96) & (lane >= 96)
    spread = (near | far).astype(BF16)
    normed, mixed = (
        jnp.concatenate([nn(a[k][...], order).astype(BF16) for a in (own, other)], axis=0)
        for k in range(2)
    )
    copies = []
    for group in range(4):
        blocks = [divmod(3 * group + k, 4) for k in range(3)]
        gqkv, g = [], []
        for gg in ggs:
            part = [gg[i][:, k * 128 : k * 128 + 128] for i, k in blocks]
            gqkv.append(jnp.concatenate(part, axis=1))
            g.append(gg[3][:, group * 128 : group * 128 + 128])
        gqkv, g = jnp.concatenate(gqkv, axis=0), jnp.concatenate(g, axis=0)
        total = jnp.concatenate([tn(normed, gqkv), tn(mixed, g)], axis=1).astype(BF16)
        total = nn(total, spread).astype(BF16)
        for xz in range(8):
            for y in range(4):
                piece = total[xz * 32 : xz * 32 + 32, y * 128 : y * 128 + 128]
                made[(xz >> 1) * 4 + y, group * 2 + (xz & 1)] = piece
        zs = pl.ds(group * 2, 2)
        copies.append(
            pltpu.make_async_copy(made.at[:, zs], out_ref.at[:, zs], sems.at[group])
        )
        copies[-1].start()
    for copy in copies:
        copy.wait()


WHOLE = pl.BlockSpec()
ANY = pl.BlockSpec(memory_space=pl.ANY)
HELD = pl.BlockSpec(memory_space=pltpu.VMEM)
SMEM = pl.BlockSpec(memory_space=pltpu.SMEM)
MIB = 2**20
ROOM = 60


def shape(*dims, dtype=BF16):
    return jax.ShapeDtypeStruct(dims, dtype)


def costs(args, outs, flops):
    nbytes = 1 if flops == 1 else sum(a.size * a.dtype.itemsize for a in (*args, *outs))
    return pl.CostEstimate(flops=flops, bytes_accessed=nbytes, transcendentals=0)


def call(kernel, outs, specs, args, room=8):
    return pl.pallas_call(
        kernel,
        out_shape=outs,
        in_specs=specs,
        out_specs=[WHOLE] * len(outs),
        compiler_params=pltpu.CompilerParams(vmem_limit_bytes=room * MIB),
        cost_estimate=costs(args, outs, 1),
    )(*args)


def stream(kernel, outs, args, flops=1, at=None, kept=()):
    first, n, m = int(at is not None), len(args), len(outs)

    def body(*refs):
        ins, results = refs[first : first + n], refs[first + n : first + n + m]
        scratch = refs[first + n + m :]
        made, here = scratch[:m], scratch[m : m + n]
        in_sem, out_sem = refs[-2:]
        arrive = {i: pltpu.make_async_copy(ins[i], here[i], in_sem.at[i]) for i in range(n)}
        leave = {
            j: pltpu.make_async_copy(made[j], results[j], out_sem.at[j])
            for j in range(m)
            if j not in kept
        }
        for copy in arrive.values():
            copy.start()

        def take(i):
            if i in arrive:
                arrive.pop(i).wait()
            return here[i]

        def give(j, value):
            if j in kept:
                results[j][...] = value
            else:
                made[j][...] = value
                leave[j].start()

        kernel(*refs[:first], take, give)
        for copy in leave.values():
            copy.wait()

    buffers = [pltpu.VMEM(a.shape, a.dtype) for a in (*outs, *args)]
    sems = [pltpu.SemaphoreType.DMA((n,)), pltpu.SemaphoreType.DMA((m,))]
    return pl.pallas_call(
        body,
        out_shape=outs,
        in_specs=[SMEM] * first + [ANY] * n,
        out_specs=[HELD if j in kept else ANY for j in range(m)],
        scratch_shapes=buffers + sems,
        compiler_params=pltpu.CompilerParams(vmem_limit_bytes=ROOM * MIB),
        cost_estimate=costs(args, outs, flops),
    )(*([at] if first else []), *args)


def weight_terms(at, factors):
    out = shape(16, 8, 32, 128)
    return pl.pallas_call(
        weights_kernel,
        out_shape=out,
        in_specs=[SMEM] + [WHOLE] * 6 + [HELD] * 6,
        out_specs=ANY,
        scratch_shapes=[pltpu.VMEM(out.shape, BF16), pltpu.SemaphoreType.DMA((4,))],
        compiler_params=pltpu.CompilerParams(vmem_limit_bytes=16 * MIB),
        cost_estimate=costs(factors, (out,), 1),
    )(at, *factors, *map(swap_cores, factors))


def swap_cores(values):
    return lax.ppermute(values, "core", [(0, 1), (1, 0)])


def a2a(values, axes):
    return lax.all_to_all(values, axes, split_axis=0, concat_axis=0, tiled=True)


def around(parts, axis):
    n = len(parts)
    return [parts[0]] + [
        lax.ppermute(parts[k], axis, [(i, (i + k) % n) for i in range(n)]) for k in range(1, n)
    ]


def first_hop(parts):
    axes = ("zh", "core")
    return [parts[0]] + [
        lax.ppermute(parts[zc], axes, [(i, i ^ zc) for i in range(4)]) for zc in range(1, 4)
    ]


def regroup(parts):
    return call(regroup_kernel, [shape(64, CH)] * len(parts), [WHOLE] * len(parts), parts)


def together(*values):
    return lax.optimization_barrier(values)


def line_sum(values):
    return jnp.sum(values.astype(F32), axis=0).astype(BF16)


def on_device(latent, grad_latent, w_qkv_row, w_out_row, w_qkv_col, w_out_col):
    at = [lax.axis_index(name) for name in ("x", "zh", "core", "zl", "y")]
    at = jnp.stack(at).astype(jnp.int32)
    cells, sent = shape(256, CH), shape(256, 2, 256)
    grad_latent = grad_latent.reshape(256, CH)
    g_col = call(pack_kernel, [shape(64, CH)] * 4, [SMEM, WHOLE], (at, grad_latent))
    g_col = first_hop(g_col)
    x_row = a2a(latent, COL).reshape(256, CH)
    (mid_row,) = stream(
        forward_kernel, [sent], (x_row, w_qkv_row, w_out_row), 10**9
    )
    mid_row, g_col = together(mid_row, g_col)
    g_col = around(regroup(g_col), "x")
    x_col = a2a(mid_row, ROW + COL)
    gx_col, *parts = stream(
        both_kernel,
        [sent] + [shape(64, CH)] * 4 + [cells] * 6,
        (x_col, w_qkv_col, w_out_col, *g_col),
        3 * 10**9,
        at,
    )
    y_col, factors_c = parts[:4], parts[4:]
    g_row = a2a(gx_col, ROW + COL)
    terms = weight_terms(at, factors_c)
    late_x, gx_col = together(x_row, gx_col)
    normed_r, scale_r, qkn_r, v_r, q_t_r, weights_r, mixed_r = stream(
        recall_kernel,
        [
            cells,
            shape(256, 128, dtype=F32),
            shape(256, 2 * CH),
            cells,
            shape(CH, 256),
            shape(HEADS, 256, 256),
            cells,
        ],
        (late_x, w_qkv_row),
    )
    g_row, terms, qkn_r = together(g_row, terms, qkn_r)
    parts = stream(
        back_kernel,
        [shape(64, CH)] * 4 + [cells] * 4,
        (g_row, w_out_row, v_r, weights_r, mixed_r, qkn_r, q_t_r, scale_r, x_row, w_qkv_row),
        2 * 10**9,
        at,
        (4, 5, 6, 7),
    )
    sums_c = a2a(terms, ("x", "y"))
    gx_row = parts[:4]
    terms = weight_terms(at, [normed_r, mixed_r, *parts[4:]])
    sums_c, terms = together(sums_c, terms)
    sums_r = a2a(terms, ("x", "y"))
    gx_row = around(gx_row, "zl")
    y_col = first_hop(y_col)
    sums = jnp.stack([line_sum(sums_r), line_sum(sums_c)], axis=1)
    sums, *parts = together(sums, *y_col, *gx_row)
    sums = a2a(sums, ("zl", "zh"))
    parts = regroup(parts)
    parts = around(parts[:4], "x") + around(parts[4:], "y")
    final, grad_input = call(unpack_kernel, [cells] * 2, [SMEM] + [WHOLE] * 8, (at, *parts))
    final, grad_input = final.reshape(16, 16, CH), grad_input.reshape(16, 16, CH)
    gq, go = shape(32, 96, dtype=F32), shape(32, 32, dtype=F32)
    grads = call(finish_kernel, [gq, go] * 2, [WHOLE], (sums,))
    return (final, grad_input, *grads)


def solution(mesh):
    fine = Mesh(mesh.devices.reshape(4, 2, 2, 4, 4), ("x", "zh", "core", "zl", "y"))
    in_specs = (P(ROW, COL, None), P(ROW, COL, None), P(), P(), P(), P())
    out_specs = (
        P(ROW, COL, None),
        P(ROW, COL, None),
        P(ROW, COL),
        P(ROW, COL),
        P(ROW, COL),
        P(ROW, COL),
    )
    return jax.shard_map(
        on_device, mesh=fine, in_specs=in_specs, out_specs=out_specs, check_vma=False
    )
```

```python
import functools

import jax
import jax.numpy as jnp
from jax import lax
from jax.experimental import pallas as pl
from jax.experimental.pallas import tpu as pltpu
from jax.sharding import Mesh
from jax.sharding import PartitionSpec as P

HEADS = 8
HD = 64
CH = 512
EPS = 1e-06
F32 = jnp.float32
BF16 = jnp.bfloat16

ROW = ("x", "zh", "core")
COL = ("zl", "y")


def nn(a, b):
    return jnp.dot(a, b, preferred_element_type=F32)


def nt(a, b):
    return lax.dot_general(a, b, (((1,), (1,)), ((), ())), preferred_element_type=F32)


def tn(a, b):
    return lax.dot_general(a, b, (((0,), (0,)), ((), ())), preferred_element_type=F32)


def iota(shape, dim):
    return lax.broadcasted_iota(jnp.int32, shape, dim)


def head_map():
    shape = (2 * CH, 128)
    lane = iota(shape, 1)
    return ((iota(shape, 0) // HD == (lane & 15)) & (lane < 32)).astype(BF16)


def head_mean(values, heads):
    return nn(values.astype(BF16), heads) * (1.0 / HD)


def head_spread(values, heads):
    high = values.astype(BF16)
    rest = (values - high.astype(F32)).astype(BF16)
    lane = iota(values.shape, 1)
    return nt(jnp.where(lane < 16, high, rest), heads)


def inv_rms(x):
    return lax.rsqrt(jnp.mean(x * x, axis=-1, keepdims=True) + EPS)


def swap_order(values):
    rows = iota((256, 256), 0)
    cols = iota((256, 256), 1)
    swap = ((rows & 15) * 16 + (rows >> 4) == cols).astype(BF16)
    return nn(swap, values).astype(BF16)


def rows_from(source, values):
    return nn((iota((256, 256), 1) == source).astype(BF16), values).astype(BF16)


def pack_rows(values, device, inner_first):
    row = iota((256, 256), 0)
    to, cell = device(row >> 6, (row >> 4) & 3), row & 15
    packed = rows_from(to * 16 + cell if inner_first else cell * 16 + to, values)
    return [packed[k * 64 : k * 64 + 64] for k in range(4)]


def unpack_rows(refs, away, cell_first):
    row = iota((256, 256), 0)
    device, cell = (row & 15, row >> 4) if cell_first else (row >> 4, row & 15)
    one, two = away(device)
    values = jnp.concatenate([ref[...] for ref in refs], axis=0)
    return rows_from(two * 64 + one * 16 + cell, values)


def row_device(at_ref, one, two):
    return ((at_ref[0] + two) & 3) * 4 + (one ^ (at_ref[1] * 2 + at_ref[2]))


def row_away(at_ref, device):
    return (device & 3) ^ (at_ref[1] * 2 + at_ref[2]), (at_ref[0] - (device >> 2)) & 3


def turned_device(at_ref, one, two):
    return row_device(at_ref, two, one)


def turned_away(at_ref, device):
    return row_away(at_ref, device)[::-1]


def col_device(at_ref, one, two):
    return ((at_ref[3] + one) & 3) * 4 + ((at_ref[4] + two) & 3)


def col_away(at_ref, device):
    return (at_ref[3] - (device >> 2)) & 3, (at_ref[4] - (device & 3)) & 3


def pack_kernel(at_ref, g_ref, *refs):
    parts = pack_rows(g_ref[...], functools.partial(row_device, at_ref), False)
    for ref, part in zip(refs, parts):
        ref[...] = part


def unpack_kernel(at_ref, *refs):
    refs[8][...] = unpack_rows(refs[:4], functools.partial(turned_away, at_ref), True)
    refs[9][...] = unpack_rows(refs[4:8], functools.partial(col_away, at_ref), False)


def regroup_kernel(*refs):
    n = len(refs) // 2
    for first in range(0, n, 4):
        for two in range(4):
            for one in range(4):
                part = refs[first + one][two * 16 : two * 16 + 16]
                refs[n + first + two][one * 16 : one * 16 + 16] = part


def project(x, w_qkv, heads):
    normed = (x * inv_rms(x)).astype(BF16)
    qkv = nn(normed, w_qkv[...])
    qk = qkv[:, : 2 * CH]
    scale = lax.rsqrt(head_mean(qk * qk, heads) + EPS)
    qkn = (qk * head_spread(scale, heads)).astype(BF16)
    return normed, scale, qkn, qkv[:, 2 * CH :].astype(BF16)


def low_half():
    return iota((256, 128), 1) < HD


def only(half, values):
    low = low_half()
    keep = low if half == 0 else jnp.logical_not(low)
    return jnp.where(keep, values, jnp.zeros_like(values))


def softmax(query, keys):
    expo = jnp.exp(nt(query, keys) * 0.125)
    return expo * (1.0 / jnp.sum(expo, axis=-1, keepdims=True))


def attend(qkn, v, pair):
    at = slice(pair * 128, pair * 128 + 128)
    q2, k2, v2 = qkn[:, at], qkn[:, CH + pair * 128 : CH + pair * 128 + 128], v[:, at]
    parts = [nn(softmax(only(h, q2), k2).astype(BF16), v2) for h in range(2)]
    return jnp.where(low_half(), parts[0], parts[1])


def attend_back(qkn, v, gmix, gmix_t, q_t, pair, recalled):
    at = slice(pair * 128, pair * 128 + 128)
    q2, k2, v2 = qkn[:, at], qkn[:, CH + pair * 128 : CH + pair * 128 + 128], v[:, at]
    g2 = gmix[:, at]
    g2f = g2.astype(F32)
    low = low_half()
    mix, gq, gk, gv = [], [], [], []
    for h in range(2):
        rows = slice(pair * 128 + h * HD, pair * 128 + h * HD + HD)
        if recalled is None:
            weights = softmax(only(h, q2), k2)
            rounded = weights.astype(BF16)
            mix.append(nn(rounded, v2))
            inner = jnp.sum(only(h, g2f * mix[h]), axis=-1, keepdims=True)
        else:
            rounded = recalled[0][2 * pair + h]
            weights = rounded.astype(F32)
            inner = jnp.sum(only(h, g2f * recalled[1][:, at].astype(F32)), axis=-1, keepdims=True)
        gweights = nt(only(h, g2), v2)
        gscores = (weights * (gweights - inner) * 0.125).astype(BF16)
        gv.append(nn(gmix_t[rows], rounded))
        gq.append(nn(gscores, k2))
        gk.append(nn(q_t[rows], gscores))
    return (
        jnp.where(low, mix[0], mix[1]) if recalled is None else None,
        jnp.where(low, gq[0], gq[1]),
        jnp.concatenate(gk, axis=0),
        jnp.concatenate(gv, axis=0),
    )


def forward_kernel(take, give):
    x = take(0)[...].astype(F32)
    _, _, qkn, v = project(x, take(1), head_map())
    mixed = [attend(qkn, v, pair).astype(BF16) for pair in range(HEADS // 2)]
    y = (x + nn(jnp.concatenate(mixed, axis=1), take(2)[...])).astype(BF16)
    give(0, swap_order(y).reshape(256, 2, 256))


def recall_kernel(take, give):
    normed, scale, qkn, v = project(take(0)[...].astype(F32), take(1), head_map())
    give(1, scale)
    give(2, qkn)
    give(3, v)
    give(4, qkn[:, :CH].T)
    weights, mixed = [], []
    for pair in range(HEADS // 2):
        at = slice(pair * 128, pair * 128 + 128)
        q2, k2, v2 = qkn[:, at], qkn[:, CH + pair * 128 : CH + pair * 128 + 128], v[:, at]
        parts = []
        for h in range(2):
            rounded = softmax(only(h, q2), k2).astype(BF16)
            weights.append(rounded)
            parts.append(nn(rounded, v2))
        mixed.append(jnp.where(low_half(), parts[0], parts[1]).astype(BF16))
    give(0, normed)
    give(6, jnp.concatenate(mixed, axis=1))
    give(5, jnp.stack(weights))


def backward_tail(
    x, g, take_wq, scale, qkn, v, q_t, gmix, gmix_t, heads, recalled, give_terms
):
    gqs, gks, gvs, mixed = [], [], [], []
    for pair in range(HEADS // 2):
        mix, gq, gk, gv = attend_back(qkn, v, gmix, gmix_t, q_t, pair, recalled)
        if recalled is None:
            mixed.append(mix.astype(BF16))
        gqs.append(gq.astype(BF16))
        gks.append(gk.astype(BF16).T)
        gvs.append(gv.astype(BF16).T)
    gqk = jnp.concatenate(gqs + gks, axis=1).astype(F32)
    yn = qkn.astype(F32)
    inner = head_spread(head_mean(yn * gqk, heads), heads)
    gqk = head_spread(scale, heads) * (gqk - yn * inner)
    gqk = gqk.astype(BF16)
    gqkv = [gqk[:, :CH], gqk[:, CH:], jnp.concatenate(gvs, axis=1)]
    give_terms(mixed, gqkv)
    gnormed = nt(jnp.concatenate(gqkv, axis=1), take_wq()[...]).astype(BF16).astype(F32)
    r = inv_rms(x)
    xn = x * r
    gx = g + r * (gnormed - xn * jnp.mean(xn * gnormed, axis=-1, keepdims=True))
    return gx.astype(BF16), mixed


def both_kernel(at_ref, take, give):
    x = take(0)[...].astype(F32).reshape(256, CH)
    heads = head_map()
    normed, scale, qkn, v = project(x, take(1), heads)
    g = unpack_rows([take(3 + k) for k in range(4)], functools.partial(row_away, at_ref), False)
    give(5, normed)
    give(10, g)
    wo = take(2)[...]

    def give_terms(mixed, gqkv):
        give(6, jnp.concatenate(mixed, axis=1))
        for k, part in enumerate(gqkv):
            give(7 + k, part)

    gx, mixed = backward_tail(
        x,
        g.astype(F32),
        lambda: take(1),
        scale,
        qkn,
        v,
        qkn[:, :CH].T,
        nt(g, wo).astype(BF16),
        nt(wo, g).astype(BF16),
        heads,
        None,
        give_terms,
    )
    give(0, gx.reshape(256, 2, 256))
    y = (x + nn(jnp.concatenate(mixed, axis=1), wo)).astype(BF16)
    for k, part in enumerate(pack_rows(y, functools.partial(turned_device, at_ref), True)):
        give(1 + k, part)


def back_kernel(at_ref, take, give):
    g = swap_order(take(0)[...].astype(F32).reshape(256, CH).astype(BF16))
    give(7, g)
    wo = take(1)[...]
    gmix, gmix_t = nt(g, wo).astype(BF16), nt(wo, g).astype(BF16)
    v, recalled, qkn, q_t = take(2)[...], (take(3), take(4)), take(5)[...], take(6)[...]
    scale, x = take(7)[...], take(8)[...].astype(F32)
    gx, _ = backward_tail(
        x,
        g.astype(F32),
        lambda: take(9),
        scale,
        qkn,
        v,
        q_t,
        gmix,
        gmix_t,
        head_map(),
        recalled,
        lambda _, gqkv: [give(4 + k, part) for k, part in enumerate(gqkv)],
    )
    for k, part in enumerate(pack_rows(gx, functools.partial(col_device, at_ref), True)):
        give(k, part)


def finish_kernel(sums_ref, *refs):
    totals = jnp.sum(sums_ref[...].astype(F32), axis=0)
    for k in range(2):
        refs[2 * k][...] = totals[k, :, :96]
        refs[2 * k + 1][...] = totals[k, :, 96:]


def weights_kernel(at_ref, take, give):
    core = at_ref[2]
    col = iota((CH, 256), 1)
    order = (iota((CH, 256), 0) == (col >> 5) * 64 + core * 32 + (col & 31)).astype(BF16)
    row, col = iota((CH, CH), 0), iota((CH, CH), 1)
    lane = col & 127
    near = (row == (col >> 7) * 96 + lane) & (lane < 96)
    far = (row == 384 + (col >> 7) * 32 + lane - 96) & (lane >= 96)
    spread = (near | far).astype(BF16)
    normed, mixed = (
        jnp.concatenate([nn(take(k + i)[...], order).astype(BF16) for k in (0, 6)], axis=0)
        for i in range(2)
    )
    ggs = [[take(k + i) for i in range(2, 6)] for k in (0, 6)]
    for group in range(4):
        blocks = [divmod(3 * group + k, 4) for k in range(3)]
        gqkv, g = [], []
        for gg in ggs:
            part = [gg[i][:, k * 128 : k * 128 + 128] for i, k in blocks]
            gqkv.append(jnp.concatenate(part, axis=1))
            g.append(gg[3][:, group * 128 : group * 128 + 128])
        gqkv, g = jnp.concatenate(gqkv, axis=0), jnp.concatenate(g, axis=0)
        total = jnp.concatenate([tn(normed, gqkv), tn(mixed, g)], axis=1).astype(BF16)
        total = nn(total, spread).astype(BF16)
        for xz in range(8):
            for y in range(4):
                piece = total[xz * 32 : xz * 32 + 32, y * 128 : y * 128 + 128]
                give(0, piece, ((xz >> 1) * 4 + y, group * 2 + (xz & 1)))
        give(0, part=(slice(None), pl.ds(group * 2, 2)))


WHOLE = pl.BlockSpec()
ANY = pl.BlockSpec(memory_space=pl.ANY)
HELD = pl.BlockSpec(memory_space=pltpu.VMEM)
SMEM = pl.BlockSpec(memory_space=pltpu.SMEM)
MIB = 2**20
ROOM = 60


def shape(*dims, dtype=BF16):
    return jax.ShapeDtypeStruct(dims, dtype)


def costs(args, outs, flops):
    nbytes = 1 if flops == 1 else sum(a.size * a.dtype.itemsize for a in (*args, *outs))
    return pl.CostEstimate(flops=flops, bytes_accessed=nbytes, transcendentals=0)


def call(kernel, outs, specs, args, room=8):
    return pl.pallas_call(
        kernel,
        out_shape=outs,
        in_specs=specs,
        out_specs=[WHOLE] * len(outs),
        compiler_params=pltpu.CompilerParams(vmem_limit_bytes=room * MIB),
        cost_estimate=costs(args, outs, 1),
    )(*args)


def stream(kernel, outs, args, flops=1, at=None, held=()):
    first, n, m = int(at is not None), len(args), len(outs)
    moved = [i for i in range(n) if i not in held]

    def body(*refs):
        ins, results = refs[first : first + n], refs[first + n : first + n + m]
        scratch = refs[first + n + m :]
        made, here, arrive = scratch[:m], dict(enumerate(ins)), {}
        in_sem, out_sem = refs[-2:]
        for k, i in enumerate(moved):
            here[i] = scratch[m + k]
            arrive[i] = pltpu.make_async_copy(ins[i], here[i], in_sem.at[k])
        leave = []
        for copy in arrive.values():
            copy.start()

        def take(i):
            if i in arrive:
                arrive.pop(i).wait()
            return here[i]

        def give(j, value=None, place=..., part=...):
            if value is not None:
                made[j][place] = value
            if value is None or place is ...:
                sem = out_sem.at[len(leave)]
                leave.append(pltpu.make_async_copy(made[j].at[part], results[j].at[part], sem))
                leave[-1].start()

        kernel(*refs[:first], take, give)
        for copy in leave:
            copy.wait()

    buffers = [pltpu.VMEM(a.shape, a.dtype) for a in (*outs, *(args[i] for i in moved))]
    sems = [pltpu.SemaphoreType.DMA((n,)), pltpu.SemaphoreType.DMA((m + 4,))]
    return pl.pallas_call(
        body,
        out_shape=outs,
        in_specs=[SMEM] * first + [HELD if i in held else ANY for i in range(n)],
        out_specs=[ANY] * m,
        scratch_shapes=buffers + sems,
        compiler_params=pltpu.CompilerParams(vmem_limit_bytes=ROOM * MIB),
        cost_estimate=costs(args, outs, flops),
    )(*([at] if first else []), *args)


def weight_terms(at, factors):
    factors = [*factors, *map(swap_cores, factors)]
    out = [shape(16, 8, 32, 128)]
    return stream(weights_kernel, out, factors, at=at, held=range(6, 12))[0]


def swap_cores(values):
    return lax.ppermute(values, "core", [(0, 1), (1, 0)])


def a2a(values, axes):
    return lax.all_to_all(values, axes, split_axis=0, concat_axis=0, tiled=True)


def around(parts, axis):
    n = len(parts)
    return [parts[0]] + [
        lax.ppermute(parts[k], axis, [(i, (i + k) % n) for i in range(n)]) for k in range(1, n)
    ]


def bit_hop(parts):
    axes = ("zh", "core")
    return [parts[0]] + [
        lax.ppermute(parts[zc], axes, [(i, i ^ zc) for i in range(4)]) for zc in range(1, 4)
    ]


def regroup(parts):
    return call(regroup_kernel, [shape(64, CH)] * len(parts), [WHOLE] * len(parts), parts)


def together(*values):
    return lax.optimization_barrier(values)


def line_sum(values):
    return jnp.sum(values.astype(F32), axis=0).astype(BF16)


def on_device(latent, grad_latent, w_qkv_row, w_out_row, w_qkv_col, w_out_col):
    at = [lax.axis_index(name) for name in ("x", "zh", "core", "zl", "y")]
    at = jnp.stack(at).astype(jnp.int32)
    cells, sent = shape(256, CH), shape(256, 2, 256)
    grad_latent = grad_latent.reshape(256, CH)
    g_col = call(pack_kernel, [shape(64, CH)] * 4, [SMEM, WHOLE], (at, grad_latent))
    g_col = bit_hop(g_col)
    x_row = a2a(latent, COL).reshape(256, CH)
    (mid_row,) = stream(
        forward_kernel, [sent], (x_row, w_qkv_row, w_out_row), 10**9
    )
    mid_row, g_col = together(mid_row, g_col)
    g_col = around(regroup(g_col), "x")
    x_col = a2a(mid_row, ROW + COL)
    late_x, mid_row = together(x_row, mid_row)
    normed_r, scale_r, qkn_r, v_r, q_t_r, weights_r, mixed_r = stream(
        recall_kernel,
        [
            cells,
            shape(256, 128, dtype=F32),
            shape(256, 2 * CH),
            cells,
            shape(CH, 256),
            shape(HEADS, 256, 256),
            cells,
        ],
        (late_x, w_qkv_row),
    )
    x_col, qkn_r = together(x_col, qkn_r)
    gx_col, *parts = stream(
        both_kernel,
        [sent] + [shape(64, CH)] * 4 + [cells] * 6,
        (x_col, w_qkv_col, w_out_col, *g_col),
        3 * 10**9,
        at,
    )
    y_col, factors_c = parts[:4], parts[4:]
    g_row = a2a(gx_col, ROW + COL)
    terms = weight_terms(at, factors_c)
    y_col = around(y_col, "x")
    g_row, terms, *y_col = together(g_row, terms, *y_col)
    parts = stream(
        back_kernel,
        [shape(64, CH)] * 4 + [cells] * 4,
        (g_row, w_out_row, v_r, weights_r, mixed_r, qkn_r, q_t_r, scale_r, x_row, w_qkv_row),
        2 * 10**9,
        at,
    )
    sums_c = a2a(terms, ("x", "y"))
    gx_row = parts[:4]
    terms = weight_terms(at, [normed_r, mixed_r, *parts[4:]])
    sums_c, terms = together(sums_c, terms)
    sums_r = a2a(terms, ("x", "y"))
    gx_row = around(gx_row, "zl")
    y_col = bit_hop(regroup(y_col))
    sums = jnp.stack([line_sum(sums_r), line_sum(sums_c)], axis=1)
    sums, *parts = together(sums, *y_col, *gx_row)
    sums = a2a(sums, ("zl", "zh"))
    parts = parts[:4] + around(regroup(parts[4:]), "y")
    final, grad_input = call(unpack_kernel, [cells] * 2, [SMEM] + [WHOLE] * 8, (at, *parts))
    final, grad_input = final.reshape(16, 16, CH), grad_input.reshape(16, 16, CH)
    gq, go = shape(32, 96, dtype=F32), shape(32, 32, dtype=F32)
    grads = call(finish_kernel, [gq, go] * 2, [WHOLE], (sums,))
    return (final, grad_input, *grads)


def solution(mesh):
    fine = Mesh(mesh.devices.reshape(4, 2, 2, 4, 4), ("x", "zh", "core", "zl", "y"))
    in_specs = (P(ROW, COL, None), P(ROW, COL, None), P(), P(), P(), P())
    out_specs = (
        P(ROW, COL, None),
        P(ROW, COL, None),
        P(ROW, COL),
        P(ROW, COL),
        P(ROW, COL),
        P(ROW, COL),
    )
    return jax.shard_map(
        on_device, mesh=fine, in_specs=in_specs, out_specs=out_specs, check_vma=False
    )
```

```python
import functools

import jax
import jax.numpy as jnp
from jax import lax
from jax.experimental import pallas as pl
from jax.experimental.pallas import tpu as pltpu
from jax.sharding import Mesh
from jax.sharding import PartitionSpec as P

HEADS = 8
HD = 64
CH = 512
EPS = 1e-06
F32 = jnp.float32
BF16 = jnp.bfloat16

ROW = ("x", "zh", "core")
COL = ("zl", "y")


def nn(a, b):
    return jnp.dot(a, b, preferred_element_type=F32)


def nt(a, b):
    return lax.dot_general(a, b, (((1,), (1,)), ((), ())), preferred_element_type=F32)


def tn(a, b):
    return lax.dot_general(a, b, (((0,), (0,)), ((), ())), preferred_element_type=F32)


def iota(shape, dim):
    return lax.broadcasted_iota(jnp.int32, shape, dim)


def head_means(values):
    low, parts = low_half(), []
    for at in range(0, 2 * CH, 128):
        pair = values[:, at : at + 128]
        first = jnp.sum(jnp.where(low, pair, 0.0), axis=-1, keepdims=True)
        second = jnp.sum(jnp.where(low, 0.0, pair), axis=-1, keepdims=True)
        parts.append(jnp.where(low, first, second))
    return jnp.concatenate(parts, axis=1) * (1.0 / HD)


def inv_rms(x):
    return lax.rsqrt(jnp.mean(x * x, axis=-1, keepdims=True) + EPS)


def swap_order(values):
    rows = iota((256, 256), 0)
    cols = iota((256, 256), 1)
    swap = ((rows & 15) * 16 + (rows >> 4) == cols).astype(BF16)
    return nn(swap, values).astype(BF16)


def rows_from(source, values):
    return nn((iota((256, 256), 1) == source).astype(BF16), values).astype(BF16)


def pack_rows(values, device, inner_first):
    row = iota((256, 256), 0)
    to, cell = device(row >> 6, (row >> 4) & 3), row & 15
    packed = rows_from(to * 16 + cell if inner_first else cell * 16 + to, values)
    return [packed[k * 64 : k * 64 + 64] for k in range(4)]


def unpack_rows(refs, away, cell_first):
    row = iota((256, 256), 0)
    device, cell = (row & 15, row >> 4) if cell_first else (row >> 4, row & 15)
    one, two = away(device)
    values = jnp.concatenate([ref[...] for ref in refs], axis=0)
    return rows_from(two * 64 + one * 16 + cell, values)


def row_device(at_ref, one, two):
    return ((at_ref[0] + two) & 3) * 4 + (one ^ (at_ref[1] * 2 + at_ref[2]))


def row_away(at_ref, device):
    return (device & 3) ^ (at_ref[1] * 2 + at_ref[2]), (at_ref[0] - (device >> 2)) & 3


def turned_device(at_ref, one, two):
    return row_device(at_ref, two, one)


def turned_away(at_ref, device):
    return row_away(at_ref, device)[::-1]


def col_device(at_ref, one, two):
    return ((at_ref[3] + one) & 3) * 4 + ((at_ref[4] + two) & 3)


def col_away(at_ref, device):
    return (at_ref[3] - (device >> 2)) & 3, (at_ref[4] - (device & 3)) & 3


def pack_kernel(at_ref, g_ref, *refs):
    parts = pack_rows(g_ref[...], functools.partial(row_device, at_ref), False)
    for ref, part in zip(refs, parts):
        ref[...] = part


def unpack_kernel(at_ref, *refs):
    refs[8][...] = unpack_rows(refs[:4], functools.partial(turned_away, at_ref), True)
    refs[9][...] = unpack_rows(refs[4:8], functools.partial(col_away, at_ref), False)


def regroup_kernel(*refs):
    n = len(refs) // 2
    for first in range(0, n, 4):
        for two in range(4):
            for one in range(4):
                part = refs[first + one][two * 16 : two * 16 + 16]
                refs[n + first + two][one * 16 : one * 16 + 16] = part


def project(x, w_qkv):
    normed = (x * inv_rms(x)).astype(BF16)
    qkv = nn(normed, w_qkv[...])
    qk = qkv[:, : 2 * CH]
    scale = lax.rsqrt(head_means(qk * qk) + EPS)
    qkn = (qk * scale).astype(BF16)
    return normed, scale, qkn, qkv[:, 2 * CH :].astype(BF16)


def low_half():
    return iota((256, 128), 1) < HD


def only(half, values):
    low = low_half()
    keep = low if half == 0 else jnp.logical_not(low)
    return jnp.where(keep, values, jnp.zeros_like(values))


def softmax(query, keys):
    expo = jnp.exp(nt(query, keys) * 0.125)
    return expo * (1.0 / jnp.sum(expo, axis=-1, keepdims=True))


def attend(qkn, v, pair):
    at = slice(pair * 128, pair * 128 + 128)
    q2, k2, v2 = qkn[:, at], qkn[:, CH + pair * 128 : CH + pair * 128 + 128], v[:, at]
    parts = [nn(softmax(only(h, q2), k2).astype(BF16), v2) for h in range(2)]
    return jnp.where(low_half(), parts[0], parts[1])


def attend_back(qkn, v, gmix, pair, recalled):
    at = slice(pair * 128, pair * 128 + 128)
    q2, k2, v2 = qkn[:, at], qkn[:, CH + pair * 128 : CH + pair * 128 + 128], v[:, at]
    g2 = gmix[:, at]
    g2f = g2.astype(F32)
    low = low_half()
    mix, gq, gk, gv = [], [], [], []
    for h in range(2):
        if recalled is None:
            weights = softmax(only(h, q2), k2)
            rounded = weights.astype(BF16)
            mix.append(nn(rounded, v2))
            inner = jnp.sum(only(h, g2f * mix[h]), axis=-1, keepdims=True)
        else:
            rounded = recalled[0][2 * pair + h]
            weights = rounded.astype(F32)
            inner = jnp.sum(only(h, g2f * recalled[1][:, at].astype(F32)), axis=-1, keepdims=True)
        gweights = nt(only(h, g2), v2)
        gscores = (weights * (gweights - inner) * 0.125).astype(BF16)
        gv.append(tn(rounded, g2))
        gq.append(nn(gscores, k2))
        gk.append(tn(gscores, q2))
    return (
        jnp.where(low, mix[0], mix[1]) if recalled is None else None,
        jnp.where(low, gq[0], gq[1]),
        jnp.where(low, gk[0], gk[1]),
        jnp.where(low, gv[0], gv[1]),
    )


def forward_kernel(take, give):
    x = take(0)[...].astype(F32)
    _, _, qkn, v = project(x, take(1))
    mixed = [attend(qkn, v, pair).astype(BF16) for pair in range(HEADS // 2)]
    y = (x + nn(jnp.concatenate(mixed, axis=1), take(2)[...])).astype(BF16)
    give(0, swap_order(y).reshape(256, 2, 256))


def recall_kernel(take, give):
    normed, scale, qkn, v = project(take(0)[...].astype(F32), take(1))
    give(1, scale)
    give(2, qkn)
    give(3, v)
    weights, mixed = [], []
    for pair in range(HEADS // 2):
        at = slice(pair * 128, pair * 128 + 128)
        q2, k2, v2 = qkn[:, at], qkn[:, CH + pair * 128 : CH + pair * 128 + 128], v[:, at]
        parts = []
        for h in range(2):
            rounded = softmax(only(h, q2), k2).astype(BF16)
            weights.append(rounded)
            parts.append(nn(rounded, v2))
        mixed.append(jnp.where(low_half(), parts[0], parts[1]).astype(BF16))
    give(0, normed)
    give(5, jnp.concatenate(mixed, axis=1))
    give(4, jnp.stack(weights))


def backward_tail(
    x, g, take_wq, scale, qkn, v, gmix, recalled, give_terms
):
    gqs, gks, gvs, mixed = [], [], [], []
    for pair in range(HEADS // 2):
        mix, gq, gk, gv = attend_back(qkn, v, gmix, pair, recalled)
        if recalled is None:
            mixed.append(mix.astype(BF16))
        gqs.append(gq.astype(BF16))
        gks.append(gk.astype(BF16))
        gvs.append(gv.astype(BF16))
    gqk = jnp.concatenate(gqs + gks, axis=1).astype(F32)
    yn = qkn.astype(F32)
    gqk = scale * (gqk - yn * head_means(yn * gqk))
    gqk = gqk.astype(BF16)
    gqkv = [gqk[:, :CH], gqk[:, CH:], jnp.concatenate(gvs, axis=1)]
    give_terms(mixed, gqkv)
    gnormed = nt(jnp.concatenate(gqkv, axis=1), take_wq()[...]).astype(BF16).astype(F32)
    r = inv_rms(x)
    xn = x * r
    gx = g + r * (gnormed - xn * jnp.mean(xn * gnormed, axis=-1, keepdims=True))
    return gx.astype(BF16), mixed


def both_kernel(at_ref, take, give):
    x = take(0)[...].astype(F32).reshape(256, CH)
    normed, scale, qkn, v = project(x, take(1))
    g = unpack_rows([take(3 + k) for k in range(4)], functools.partial(row_away, at_ref), False)
    give(5, normed)
    give(10, g)
    wo = take(2)[...]

    def give_terms(mixed, gqkv):
        give(6, jnp.concatenate(mixed, axis=1))
        for k, part in enumerate(gqkv):
            give(7 + k, part)

    gx, mixed = backward_tail(
        x,
        g.astype(F32),
        lambda: take(1),
        scale,
        qkn,
        v,
        nt(g, wo).astype(BF16),
        None,
        give_terms,
    )
    give(0, gx.reshape(256, 2, 256))
    y = (x + nn(jnp.concatenate(mixed, axis=1), wo)).astype(BF16)
    for k, part in enumerate(pack_rows(y, functools.partial(turned_device, at_ref), True)):
        give(1 + k, part)


def back_kernel(at_ref, take, give):
    g = swap_order(take(0)[...].astype(F32).reshape(256, CH).astype(BF16))
    give(7, g)
    wo = take(1)[...]
    gmix = nt(g, wo).astype(BF16)
    v, recalled, qkn = take(2)[...], (take(3), take(4)), take(5)[...]
    scale, x = take(6)[...], take(7)[...].astype(F32)
    gx, _ = backward_tail(
        x,
        g.astype(F32),
        lambda: take(8),
        scale,
        qkn,
        v,
        gmix,
        recalled,
        lambda _, gqkv: [give(4 + k, part) for k, part in enumerate(gqkv)],
    )
    for k, part in enumerate(pack_rows(gx, functools.partial(col_device, at_ref), True)):
        give(k, part)


def finish_kernel(sums_ref, *refs):
    totals = jnp.sum(sums_ref[...].astype(F32), axis=0)
    for k in range(2):
        refs[2 * k][...] = totals[k, :, :96]
        refs[2 * k + 1][...] = totals[k, :, 96:]


def weights_kernel(at_ref, take, give):
    core = at_ref[2]
    col = iota((CH, 256), 1)
    order = (iota((CH, 256), 0) == (col >> 5) * 64 + core * 32 + (col & 31)).astype(BF16)
    row, col = iota((CH, CH), 0), iota((CH, CH), 1)
    lane = col & 127
    near = (row == (col >> 7) * 96 + lane) & (lane < 96)
    far = (row == 384 + (col >> 7) * 32 + lane - 96) & (lane >= 96)
    spread = (near | far).astype(BF16)
    normed, mixed = (
        jnp.concatenate([nn(take(k + i)[...], order).astype(BF16) for k in (0, 6)], axis=0)
        for i in range(2)
    )
    ggs = [[take(k + i) for i in range(2, 6)] for k in (0, 6)]
    for group in range(4):
        blocks = [divmod(3 * group + k, 4) for k in range(3)]
        gqkv, g = [], []
        for gg in ggs:
            part = [gg[i][:, k * 128 : k * 128 + 128] for i, k in blocks]
            gqkv.append(jnp.concatenate(part, axis=1))
            g.append(gg[3][:, group * 128 : group * 128 + 128])
        gqkv, g = jnp.concatenate(gqkv, axis=0), jnp.concatenate(g, axis=0)
        total = jnp.concatenate([tn(normed, gqkv), tn(mixed, g)], axis=1).astype(BF16)
        total = nn(total, spread).astype(BF16)
        for xz in range(8):
            for y in range(4):
                piece = total[xz * 32 : xz * 32 + 32, y * 128 : y * 128 + 128]
                give(0, piece, ((xz >> 1) * 4 + y, group * 2 + (xz & 1)))
        give(0, part=(slice(None), pl.ds(group * 2, 2)))


WHOLE = pl.BlockSpec()
ANY = pl.BlockSpec(memory_space=pl.ANY)
SMEM = pl.BlockSpec(memory_space=pltpu.SMEM)
MIB = 2**20
ROOM = 63


def shape(*dims, dtype=BF16):
    return jax.ShapeDtypeStruct(dims, dtype)


def costs(args, outs, flops):
    nbytes = 1 if flops == 1 else sum(a.size * a.dtype.itemsize for a in (*args, *outs))
    return pl.CostEstimate(flops=flops, bytes_accessed=nbytes, transcendentals=0)


def call(kernel, outs, specs, args, room=8):
    return pl.pallas_call(
        kernel,
        out_shape=outs,
        in_specs=specs,
        out_specs=[WHOLE] * len(outs),
        compiler_params=pltpu.CompilerParams(vmem_limit_bytes=room * MIB),
        cost_estimate=costs(args, outs, 1),
    )(*args)


def stream(kernel, outs, args, flops=1, at=None):
    first, n, m = int(at is not None), len(args), len(outs)

    def body(*refs):
        ins, results = refs[first : first + n], refs[first + n : first + n + m]
        scratch = refs[first + n + m :]
        made, here = scratch[:m], scratch[m : m + n]
        in_sem, out_sem = refs[-2:]
        arrive = {i: pltpu.make_async_copy(ins[i], here[i], in_sem.at[i]) for i in range(n)}
        leave = []
        for copy in arrive.values():
            copy.start()

        def take(i):
            if i in arrive:
                arrive.pop(i).wait()
            return here[i]

        def give(j, value=None, place=..., part=...):
            if value is not None:
                made[j][place] = value
            if value is None or place is ...:
                sem = out_sem.at[len(leave)]
                leave.append(pltpu.make_async_copy(made[j].at[part], results[j].at[part], sem))
                leave[-1].start()

        kernel(*refs[:first], take, give)
        for copy in leave:
            copy.wait()

    buffers = [pltpu.VMEM(a.shape, a.dtype) for a in (*outs, *args)]
    sems = [pltpu.SemaphoreType.DMA((n,)), pltpu.SemaphoreType.DMA((m + 4,))]
    return pl.pallas_call(
        body,
        out_shape=outs,
        in_specs=[SMEM] * first + [ANY] * n,
        out_specs=[ANY] * m,
        scratch_shapes=buffers + sems,
        compiler_params=pltpu.CompilerParams(vmem_limit_bytes=ROOM * MIB),
        cost_estimate=costs(args, outs, flops),
    )(*([at] if first else []), *args)


def weight_terms(at, factors):
    factors = [*factors, *map(swap_cores, factors)]
    out = [shape(16, 8, 32, 128)]
    return stream(weights_kernel, out, factors, at=at)[0]


def swap_cores(values):
    return lax.ppermute(values, "core", [(0, 1), (1, 0)])


def a2a(values, axes):
    return lax.all_to_all(values, axes, split_axis=0, concat_axis=0, tiled=True)


def around(parts, axis):
    n = len(parts)
    return [parts[0]] + [
        lax.ppermute(parts[k], axis, [(i, (i + k) % n) for i in range(n)]) for k in range(1, n)
    ]


def bit_hop(parts, near=None):
    def move(zc):
        return lax.ppermute(parts[zc], ("zh", "core"), [(i, i ^ zc) for i in range(4)])

    return [parts[0], move(1) if near is None else near, move(2), move(3)]


def regroup(parts):
    return call(regroup_kernel, [shape(64, CH)] * len(parts), [WHOLE] * len(parts), parts)


def together(*values):
    return lax.optimization_barrier(values)


def line_sum(values):
    return jnp.sum(values.astype(F32), axis=0).astype(BF16)


def on_device(latent, grad_latent, w_qkv_row, w_out_row, w_qkv_col, w_out_col):
    at = [lax.axis_index(name) for name in ("x", "zh", "core", "zl", "y")]
    at = jnp.stack(at).astype(jnp.int32)
    cells, sent = shape(256, CH), shape(256, 2, 256)
    grad_latent = grad_latent.reshape(256, CH)
    g_col = call(pack_kernel, [shape(64, CH)] * 4, [SMEM, WHOLE], (at, grad_latent))
    g_col = bit_hop(g_col)
    x_row = a2a(latent, COL).reshape(256, CH)
    (mid_row,) = stream(
        forward_kernel, [sent], (x_row, w_qkv_row, w_out_row), 10**9
    )
    mid_row, g_col = together(mid_row, g_col)
    g_col = around(regroup(g_col), "x")
    x_col = a2a(mid_row, ROW + COL)
    late_x, mid_row = together(x_row, mid_row)
    normed_r, scale_r, qkn_r, v_r, weights_r, mixed_r = stream(
        recall_kernel,
        [
            cells,
            shape(256, 2 * CH, dtype=F32),
            shape(256, 2 * CH),
            cells,
            shape(HEADS, 256, 256),
            cells,
        ],
        (late_x, w_qkv_row),
    )
    x_col, qkn_r = together(x_col, qkn_r)
    gx_col, *parts = stream(
        both_kernel,
        [sent] + [shape(64, CH)] * 4 + [cells] * 6,
        (x_col, w_qkv_col, w_out_col, *g_col),
        3 * 10**9,
        at,
    )
    y_col, factors_c = parts[:4], parts[4:]
    g_row = a2a(gx_col, ROW + COL)
    terms = weight_terms(at, factors_c)
    y_col = around(y_col, "x")
    g_row, terms, *y_col = together(g_row, terms, *y_col)
    parts = stream(
        back_kernel,
        [shape(64, CH)] * 4 + [cells] * 4,
        (g_row, w_out_row, v_r, weights_r, mixed_r, qkn_r, scale_r, x_row, w_qkv_row),
        2 * 10**9,
        at,
    )
    sums_c = a2a(terms, ("x", "y"))
    gx_row = parts[:4]
    terms = weight_terms(at, [normed_r, mixed_r, *parts[4:]])
    sums_c, terms = together(sums_c, terms)
    sums_r = a2a(terms, ("x", "y"))
    y_col = regroup(y_col)
    near, *gx_row = together(swap_cores(y_col[1]), *gx_row)
    y_col = bit_hop(y_col, near)
    gx_row = around(gx_row, "zl")
    sums = jnp.stack([line_sum(sums_r), line_sum(sums_c)], axis=1)
    sums, *parts = together(sums, *y_col, *gx_row)
    sums = a2a(sums, ("zl", "zh"))
    parts = parts[:4] + around(regroup(parts[4:]), "y")
    final, grad_input = call(unpack_kernel, [cells] * 2, [SMEM] + [WHOLE] * 8, (at, *parts))
    final, grad_input = final.reshape(16, 16, CH), grad_input.reshape(16, 16, CH)
    gq, go = shape(32, 96, dtype=F32), shape(32, 32, dtype=F32)
    grads = call(finish_kernel, [gq, go] * 2, [WHOLE], (sums,))
    return (final, grad_input, *grads)


def solution(mesh):
    fine = Mesh(mesh.devices.reshape(4, 2, 2, 4, 4), ("x", "zh", "core", "zl", "y"))
    in_specs = (P(ROW, COL, None), P(ROW, COL, None), P(), P(), P(), P())
    out_specs = (
        P(ROW, COL, None),
        P(ROW, COL, None),
        P(ROW, COL),
        P(ROW, COL),
        P(ROW, COL),
        P(ROW, COL),
    )
    return jax.shard_map(
        on_device, mesh=fine, in_specs=in_specs, out_specs=out_specs, check_vma=False
    )
```

```python
import functools

import jax
import jax.numpy as jnp
from jax import lax
from jax.experimental import pallas as pl
from jax.experimental.pallas import tpu as pltpu
from jax.sharding import Mesh
from jax.sharding import PartitionSpec as P

HEADS = 8
HD = 64
CH = 512
EPS = 1e-06
F32 = jnp.float32
BF16 = jnp.bfloat16

ROW = ("x", "zh", "core")
COL = ("zl", "y")


def nn(a, b):
    return jnp.dot(a, b, preferred_element_type=F32)


def nt(a, b):
    return lax.dot_general(a, b, (((1,), (1,)), ((), ())), preferred_element_type=F32)


def tn(a, b):
    return lax.dot_general(a, b, (((0,), (0,)), ((), ())), preferred_element_type=F32)


def iota(shape, dim):
    return lax.broadcasted_iota(jnp.int32, shape, dim)


def head_means(values):
    low, parts = low_half(), []
    for at in range(0, 2 * CH, 128):
        pair = values[:, at : at + 128]
        first = jnp.sum(jnp.where(low, pair, 0.0), axis=-1, keepdims=True)
        second = jnp.sum(jnp.where(low, 0.0, pair), axis=-1, keepdims=True)
        parts.append(jnp.where(low, first, second))
    return jnp.concatenate(parts, axis=1) * (1.0 / HD)


def inv_rms(x):
    return lax.rsqrt(jnp.mean(x * x, axis=-1, keepdims=True) + EPS)


def swap_order(values):
    rows = iota((256, 256), 0)
    cols = iota((256, 256), 1)
    swap = ((rows & 15) * 16 + (rows >> 4) == cols).astype(BF16)
    return nn(swap, values).astype(BF16)


def rows_from(source, values):
    return nn((iota((256, 256), 1) == source).astype(BF16), values).astype(BF16)


def pack_rows(values, device, inner_first):
    row = iota((256, 256), 0)
    to, cell = device(row >> 6, (row >> 4) & 3), row & 15
    packed = rows_from(to * 16 + cell if inner_first else cell * 16 + to, values)
    return [packed[k * 64 : k * 64 + 64] for k in range(4)]


def unpack_rows(refs, away, cell_first):
    row = iota((256, 256), 0)
    device, cell = (row & 15, row >> 4) if cell_first else (row >> 4, row & 15)
    one, two = away(device)
    values = jnp.concatenate([ref[...] for ref in refs], axis=0)
    return rows_from(two * 64 + one * 16 + cell, values)


def row_device(at_ref, one, two):
    return ((at_ref[0] + two) & 3) * 4 + (one ^ (at_ref[1] * 2 + at_ref[2]))


def row_away(at_ref, device):
    return (device & 3) ^ (at_ref[1] * 2 + at_ref[2]), (at_ref[0] - (device >> 2)) & 3


def turned_device(at_ref, one, two):
    return row_device(at_ref, two, one)


def turned_away(at_ref, device):
    return row_away(at_ref, device)[::-1]


def col_device(at_ref, one, two):
    return ((at_ref[3] + one) & 3) * 4 + ((at_ref[4] + two) & 3)


def col_away(at_ref, device):
    return (at_ref[3] - (device >> 2)) & 3, (at_ref[4] - (device & 3)) & 3


def pack_kernel(at_ref, g_ref, *refs):
    parts = pack_rows(g_ref[...], functools.partial(row_device, at_ref), False)
    for ref, part in zip(refs, parts):
        ref[...] = part


def unpack_kernel(at_ref, *refs):
    refs[8][...] = unpack_rows(refs[:4], functools.partial(turned_away, at_ref), True)
    refs[9][...] = unpack_rows(refs[4:8], functools.partial(col_away, at_ref), False)


def regroup_kernel(*refs):
    n = len(refs) // 2
    for first in range(0, n, 4):
        for two in range(4):
            for one in range(4):
                part = refs[first + one][two * 16 : two * 16 + 16]
                refs[n + first + two][one * 16 : one * 16 + 16] = part


def project(x, w_qkv):
    normed = (x * inv_rms(x)).astype(BF16)
    qkv = nn(normed, w_qkv[...])
    qk = qkv[:, : 2 * CH]
    scale = lax.rsqrt(head_means(qk * qk) + EPS)
    qkn = (qk * scale).astype(BF16)
    return normed, scale, qkn, qkv[:, 2 * CH :].astype(BF16)


def low_half():
    return iota((256, 128), 1) < HD


def only(half, values):
    low = low_half()
    keep = low if half == 0 else jnp.logical_not(low)
    return jnp.where(keep, values, jnp.zeros_like(values))


def softmax(query, keys):
    expo = jnp.exp(nt(query, keys) * 0.125)
    return expo * (1.0 / jnp.sum(expo, axis=-1, keepdims=True))


def attend_back(qkn, v, gmix, pair, recalled):
    at = slice(pair * 128, pair * 128 + 128)
    q2, k2, v2 = qkn[:, at], qkn[:, CH + pair * 128 : CH + pair * 128 + 128], v[:, at]
    g2 = gmix[:, at]
    g2f = g2.astype(F32)
    low = low_half()
    mix, gq, gk, gv = [], [], [], []
    for h in range(2):
        if recalled is None:
            weights = softmax(only(h, q2), k2)
            rounded = weights.astype(BF16)
            mix.append(nn(rounded, v2))
            inner = jnp.sum(only(h, g2f * mix[h]), axis=-1, keepdims=True)
        else:
            rounded = recalled[0][2 * pair + h]
            weights = rounded.astype(F32)
            inner = jnp.sum(only(h, g2f * recalled[1][:, at].astype(F32)), axis=-1, keepdims=True)
        gweights = nt(only(h, g2), v2)
        gscores = (weights * (gweights - inner) * 0.125).astype(BF16)
        gv.append(tn(rounded, g2))
        gq.append(nn(gscores, k2))
        gk.append(tn(gscores, q2))
    return (
        jnp.where(low, mix[0], mix[1]) if recalled is None else None,
        jnp.where(low, gq[0], gq[1]),
        jnp.where(low, gk[0], gk[1]),
        jnp.where(low, gv[0], gv[1]),
    )


def forward_kernel(take, give):
    x = take(0)[...].astype(F32)
    normed, scale, qkn, v = project(x, take(1))
    give(1, normed)
    give(2, scale)
    give(3, qkn)
    give(4, v)
    weights, mixed = [], []
    for pair in range(HEADS // 2):
        at = slice(pair * 128, pair * 128 + 128)
        q2, k2, v2 = qkn[:, at], qkn[:, CH + pair * 128 : CH + pair * 128 + 128], v[:, at]
        parts = []
        for h in range(2):
            rounded = softmax(only(h, q2), k2).astype(BF16)
            weights.append(rounded)
            parts.append(nn(rounded, v2))
        mixed.append(jnp.where(low_half(), parts[0], parts[1]).astype(BF16))
    give(5, jnp.stack(weights))
    mixed = jnp.concatenate(mixed, axis=1)
    give(6, mixed)
    y = (x + nn(mixed, take(2)[...])).astype(BF16)
    give(0, swap_order(y).reshape(256, 2, 256))


def backward_tail(
    x, g, take_wq, scale, qkn, v, gmix, recalled, give_terms
):
    gqs, gks, gvs, mixed = [], [], [], []
    for pair in range(HEADS // 2):
        mix, gq, gk, gv = attend_back(qkn, v, gmix, pair, recalled)
        if recalled is None:
            mixed.append(mix.astype(BF16))
        gqs.append(gq.astype(BF16))
        gks.append(gk.astype(BF16))
        gvs.append(gv.astype(BF16))
    gqk = jnp.concatenate(gqs + gks, axis=1).astype(F32)
    yn = qkn.astype(F32)
    gqk = scale * (gqk - yn * head_means(yn * gqk))
    gqk = gqk.astype(BF16)
    gqkv = [gqk[:, :CH], gqk[:, CH:], jnp.concatenate(gvs, axis=1)]
    give_terms(mixed, gqkv)
    gnormed = nt(jnp.concatenate(gqkv, axis=1), take_wq()[...]).astype(BF16).astype(F32)
    r = inv_rms(x)
    xn = x * r
    gx = g + r * (gnormed - xn * jnp.mean(xn * gnormed, axis=-1, keepdims=True))
    return gx.astype(BF16), mixed


def both_kernel(at_ref, take, give):
    x = take(0)[...].astype(F32).reshape(256, CH)
    normed, scale, qkn, v = project(x, take(1))
    g = unpack_rows([take(3 + k) for k in range(4)], functools.partial(row_away, at_ref), False)
    give(5, normed, (slice(None), slice(0, CH)))
    give(6, g, (slice(None), slice(3 * CH, 4 * CH)))
    wo = take(2)[...]

    def give_terms(mixed, gqkv):
        give(5, jnp.concatenate(mixed, axis=1), (slice(None), slice(CH, 2 * CH)))
        give(5)
        for k, part in enumerate(gqkv):
            give(6, part, (slice(None), slice(k * CH, k * CH + CH)))
        give(6)

    gx, mixed = backward_tail(
        x,
        g.astype(F32),
        lambda: take(1),
        scale,
        qkn,
        v,
        nt(g, wo).astype(BF16),
        None,
        give_terms,
    )
    give(0, gx.reshape(256, 2, 256))
    y = (x + nn(jnp.concatenate(mixed, axis=1), wo)).astype(BF16)
    for k, part in enumerate(pack_rows(y, functools.partial(turned_device, at_ref), True)):
        give(1 + k, part)


def back_kernel(at_ref, take, give):
    g = swap_order(take(0)[...].astype(F32).reshape(256, CH).astype(BF16))
    give(7, g)
    wo = take(1)[...]
    gmix = nt(g, wo).astype(BF16)
    v, recalled, qkn = take(2)[...], (take(3), take(4)), take(5)[...]
    scale, x = take(6)[...], take(7)[...].astype(F32)
    gx, _ = backward_tail(
        x,
        g.astype(F32),
        lambda: take(8),
        scale,
        qkn,
        v,
        gmix,
        recalled,
        lambda _, gqkv: [give(4 + k, part) for k, part in enumerate(gqkv)],
    )
    for k, part in enumerate(pack_rows(gx, functools.partial(col_device, at_ref), True)):
        give(k, part)


def finish_kernel(sums_ref, *refs):
    totals = jnp.sum(sums_ref[...].astype(F32), axis=0)
    for k in range(2):
        refs[2 * k][...] = totals[k, :, :96]
        refs[2 * k + 1][...] = totals[k, :, 96:]


def weights_kernel(at_ref, take, give):
    core = at_ref[2]
    col = iota((CH, 256), 1)
    order = (iota((CH, 256), 0) == (col >> 5) * 64 + core * 32 + (col & 31)).astype(BF16)
    row, col = iota((CH, CH), 0), iota((CH, CH), 1)
    lane = col & 127
    near = (row == (col >> 7) * 96 + lane) & (lane < 96)
    far = (row == 384 + (col >> 7) * 32 + lane - 96) & (lane >= 96)
    spread = (near | far).astype(BF16)
    normed, mixed = (
        jnp.concatenate([nn(take(2 * i + k)[...], order).astype(BF16) for k in (0, 1)], axis=0)
        for i in range(2)
    )
    ggs = [[take(2 * i + k) for i in range(2, 6)] for k in (0, 1)]
    for group in range(4):
        blocks = [divmod(3 * group + k, 4) for k in range(3)]
        gqkv, g = [], []
        for gg in ggs:
            part = [gg[i][:, k * 128 : k * 128 + 128] for i, k in blocks]
            gqkv.append(jnp.concatenate(part, axis=1))
            g.append(gg[3][:, group * 128 : group * 128 + 128])
        gqkv, g = jnp.concatenate(gqkv, axis=0), jnp.concatenate(g, axis=0)
        total = jnp.concatenate([tn(normed, gqkv), tn(mixed, g)], axis=1).astype(BF16)
        total = nn(total, spread).astype(BF16)
        for xz in range(8):
            for y in range(4):
                piece = total[xz * 32 : xz * 32 + 32, y * 128 : y * 128 + 128]
                give(0, piece, ((xz >> 1) * 4 + y, group * 2 + (xz & 1)))
        give(0, part=(slice(None), pl.ds(group * 2, 2)))


WHOLE = pl.BlockSpec()
ANY = pl.BlockSpec(memory_space=pl.ANY)
SMEM = pl.BlockSpec(memory_space=pltpu.SMEM)
MIB = 2**20
ROOM = 64


def shape(*dims, dtype=BF16):
    return jax.ShapeDtypeStruct(dims, dtype)


def costs(args, outs, flops):
    nbytes = 1 if flops == 1 else sum(a.size * a.dtype.itemsize for a in (*args, *outs))
    return pl.CostEstimate(flops=flops, bytes_accessed=nbytes, transcendentals=0)


def call(kernel, outs, specs, args, room=8):
    return pl.pallas_call(
        kernel,
        out_shape=outs,
        in_specs=specs,
        out_specs=[WHOLE] * len(outs),
        compiler_params=pltpu.CompilerParams(vmem_limit_bytes=room * MIB),
        cost_estimate=costs(args, outs, 1),
    )(*args)


def stream(kernel, outs, args, flops=1, at=None, room=ROOM):
    first, n, m = int(at is not None), len(args), len(outs)

    def body(*refs):
        ins, results = refs[first : first + n], refs[first + n : first + n + m]
        scratch = refs[first + n + m :]
        made, here = scratch[:m], scratch[m : m + n]
        in_sem, out_sem = refs[-2:]
        arrive = {i: pltpu.make_async_copy(ins[i], here[i], in_sem.at[i]) for i in range(n)}
        leave = []
        for copy in arrive.values():
            copy.start()

        def take(i):
            if i in arrive:
                arrive.pop(i).wait()
            return here[i]

        def give(j, value=None, place=..., part=...):
            if value is not None:
                made[j][place] = value
            if value is None or place is ...:
                sem = out_sem.at[len(leave)]
                leave.append(pltpu.make_async_copy(made[j].at[part], results[j].at[part], sem))
                leave[-1].start()

        kernel(*refs[:first], take, give)
        for copy in leave:
            copy.wait()

    buffers = [pltpu.VMEM(a.shape, a.dtype) for a in (*outs, *args)]
    sems = [pltpu.SemaphoreType.DMA((n,)), pltpu.SemaphoreType.DMA((m + 4,))]
    return pl.pallas_call(
        body,
        out_shape=outs,
        in_specs=[SMEM] * first + [ANY] * n,
        out_specs=[ANY] * m,
        scratch_shapes=buffers + sems,
        compiler_params=pltpu.CompilerParams(vmem_limit_bytes=room * MIB),
        cost_estimate=costs(args, outs, flops),
    )(*([at] if first else []), *args)


def weight_terms(at, factors):
    factors = [half for own in factors for half in (own, swap_cores(own))]

    def kernel(at_ref, take, give):
        def part(i):
            k, c = divmod(i, 2)
            first, which = (0, k) if k < 2 else (2, k - 2)
            return take(first + c).at[:, which * CH : which * CH + CH]

        weights_kernel(at_ref, take if len(factors) == 12 else part, give)

    return stream(kernel, [shape(16, 8, 32, 128)], factors, at=at)[0]


def swap_cores(values):
    return lax.ppermute(values, "core", [(0, 1), (1, 0)])


def a2a(values, axes):
    return lax.all_to_all(values, axes, split_axis=0, concat_axis=0, tiled=True)


def around(parts, axis):
    n = len(parts)
    return [parts[0]] + [
        lax.ppermute(parts[k], axis, [(i, (i + k) % n) for i in range(n)]) for k in range(1, n)
    ]


def bit_hop(parts, near=None):
    def move(zc):
        return lax.ppermute(parts[zc], ("zh", "core"), [(i, i ^ zc) for i in range(4)])

    return [parts[0], move(1) if near is None else near, move(2), move(3)]


def regroup(parts):
    return call(regroup_kernel, [shape(64, CH)] * len(parts), [WHOLE] * len(parts), parts)


def together(*values):
    return lax.optimization_barrier(values)


def line_sum(values):
    return jnp.sum(values.astype(F32), axis=0).astype(BF16)


def on_device(latent, grad_latent, w_qkv_row, w_out_row, w_qkv_col, w_out_col):
    at = [lax.axis_index(name) for name in ("x", "zh", "core", "zl", "y")]
    at = jnp.stack(at).astype(jnp.int32)
    cells, sent = shape(256, CH), shape(256, 2, 256)
    grad_latent = grad_latent.reshape(256, CH)
    g_col = call(pack_kernel, [shape(64, CH)] * 4, [SMEM, WHOLE], (at, grad_latent))
    g_col = bit_hop(g_col)
    x_row = a2a(latent, COL).reshape(256, CH)
    mid_row, normed_r, scale_r, qkn_r, v_r, weights_r, mixed_r = stream(
        forward_kernel,
        [
            sent,
            cells,
            shape(256, 2 * CH, dtype=F32),
            shape(256, 2 * CH),
            cells,
            shape(HEADS, 256, 256),
            cells,
        ],
        (x_row, w_qkv_row, w_out_row),
        10**9,
        room=63,
    )
    mid_row, g_col = together(mid_row, g_col)
    g_col = around(regroup(g_col), "x")
    x_col = a2a(mid_row, ROW + COL)
    gx_col, *parts = stream(
        both_kernel,
        [sent] + [shape(64, CH)] * 4 + [shape(256, 2 * CH), shape(256, 4 * CH)],
        (x_col, w_qkv_col, w_out_col, *g_col),
        3 * 10**9,
        at,
    )
    y_col, factors_c = parts[:4], parts[4:]
    g_row = a2a(gx_col, ROW + COL)
    terms = weight_terms(at, factors_c)
    y_col = around(y_col, "x")
    g_row, terms, *y_col = together(g_row, terms, *y_col)
    parts = stream(
        back_kernel,
        [shape(64, CH)] * 4 + [cells] * 4,
        (g_row, w_out_row, v_r, weights_r, mixed_r, qkn_r, scale_r, x_row, w_qkv_row),
        2 * 10**9,
        at,
    )
    sums_c = a2a(terms, ("x", "y"))
    gx_row = parts[:4]
    terms = weight_terms(at, [normed_r, mixed_r, *parts[4:]])
    sums_c, terms = together(sums_c, terms)
    sums_r = a2a(terms, ("x", "y"))
    y_col = regroup(y_col)
    near, *gx_row = together(swap_cores(y_col[1]), *gx_row)
    y_col = bit_hop(y_col, near)
    gx_row = around(gx_row, "zl")
    sums = jnp.stack([line_sum(sums_r), line_sum(sums_c)], axis=1)
    sums, *parts = together(sums, *y_col, *gx_row)
    sums = a2a(sums, ("zl", "zh"))
    parts = parts[:4] + around(regroup(parts[4:]), "y")
    final, grad_input = call(unpack_kernel, [cells] * 2, [SMEM] + [WHOLE] * 8, (at, *parts))
    final, grad_input = final.reshape(16, 16, CH), grad_input.reshape(16, 16, CH)
    gq, go = shape(32, 96, dtype=F32), shape(32, 32, dtype=F32)
    grads = call(finish_kernel, [gq, go] * 2, [WHOLE], (sums,))
    return (final, grad_input, *grads)


def solution(mesh):
    fine = Mesh(mesh.devices.reshape(4, 2, 2, 4, 4), ("x", "zh", "core", "zl", "y"))
    in_specs = (P(ROW, COL, None), P(ROW, COL, None), P(), P(), P(), P())
    out_specs = (
        P(ROW, COL, None),
        P(ROW, COL, None),
        P(ROW, COL),
        P(ROW, COL),
        P(ROW, COL),
        P(ROW, COL),
    )
    return jax.shard_map(
        on_device, mesh=fine, in_specs=in_specs, out_specs=out_specs, check_vma=False
    )
```

```python
import functools

import jax
import jax.numpy as jnp
from jax import lax
from jax.experimental import pallas as pl
from jax.experimental.pallas import tpu as pltpu
from jax.sharding import Mesh
from jax.sharding import PartitionSpec as P

HEADS = 8
HD = 64
CH = 512
EPS = 1e-06
F32 = jnp.float32
BF16 = jnp.bfloat16

ROW = ("x", "zh", "core")
COL = ("zl", "y")


def nn(a, b):
    return jnp.dot(a, b, preferred_element_type=F32)


def nt(a, b):
    return lax.dot_general(a, b, (((1,), (1,)), ((), ())), preferred_element_type=F32)


def tn(a, b):
    return lax.dot_general(a, b, (((0,), (0,)), ((), ())), preferred_element_type=F32)


def iota(shape, dim):
    return lax.broadcasted_iota(jnp.int32, shape, dim)


def head_means(values):
    low, parts = low_half(), []
    for at in range(0, 2 * CH, 128):
        pair = values[:, at : at + 128]
        first = jnp.sum(jnp.where(low, pair, 0.0), axis=-1, keepdims=True)
        second = jnp.sum(jnp.where(low, 0.0, pair), axis=-1, keepdims=True)
        parts.append(jnp.where(low, first, second))
    return jnp.concatenate(parts, axis=1) * (1.0 / HD)


def inv_rms(x):
    return lax.rsqrt(jnp.mean(x * x, axis=-1, keepdims=True) + EPS)


def swap_order(values):
    rows = iota((256, 256), 0)
    cols = iota((256, 256), 1)
    swap = ((rows & 15) * 16 + (rows >> 4) == cols).astype(BF16)
    return nn(swap, values).astype(BF16)


def rows_from(source, values):
    return nn((iota((256, 256), 1) == source).astype(BF16), values).astype(BF16)


def pack_rows(values, device, inner_first):
    row = iota((256, 256), 0)
    to, cell = device(row >> 6, (row >> 4) & 3), row & 15
    packed = rows_from(to * 16 + cell if inner_first else cell * 16 + to, values)
    return [packed[k * 64 : k * 64 + 64] for k in range(4)]


def unpack_rows(refs, away, cell_first):
    row = iota((256, 256), 0)
    device, cell = (row & 15, row >> 4) if cell_first else (row >> 4, row & 15)
    one, two = away(device)
    values = jnp.concatenate([ref[...] for ref in refs], axis=0)
    return rows_from(two * 64 + one * 16 + cell, values)


def row_device(at_ref, one, two):
    return ((at_ref[0] + two) & 3) * 4 + (one ^ (at_ref[1] * 2 + at_ref[2]))


def row_away(at_ref, device):
    return (device & 3) ^ (at_ref[1] * 2 + at_ref[2]), (at_ref[0] - (device >> 2)) & 3


def turned_device(at_ref, one, two):
    return row_device(at_ref, two, one)


def turned_away(at_ref, device):
    return row_away(at_ref, device)[::-1]


def col_device(at_ref, one, two):
    return ((at_ref[3] + one) & 3) * 4 + ((at_ref[4] + two) & 3)


def col_away(at_ref, device):
    return (at_ref[3] - (device >> 2)) & 3, (at_ref[4] - (device & 3)) & 3


def pack_kernel(at_ref, g_ref, *refs):
    parts = pack_rows(g_ref[...], functools.partial(row_device, at_ref), False)
    for ref, part in zip(refs, parts):
        ref[...] = part


def unpack_kernel(at_ref, *refs):
    refs[8][...] = unpack_rows(refs[:4], functools.partial(turned_away, at_ref), True)
    refs[9][...] = unpack_rows(refs[4:8], functools.partial(col_away, at_ref), False)


def regroup_kernel(*refs):
    n = len(refs) // 2
    for first in range(0, n, 4):
        for two in range(4):
            for one in range(4):
                part = refs[first + one][two * 16 : two * 16 + 16]
                refs[n + first + two][one * 16 : one * 16 + 16] = part


def project(x, w_qkv):
    normed = (x * inv_rms(x)).astype(BF16)
    qkv = nn(normed, w_qkv[...])
    qk = qkv[:, : 2 * CH]
    scale = lax.rsqrt(head_means(qk * qk) + EPS)
    qkn = (qk * scale).astype(BF16)
    return normed, scale, qkn, qkv[:, 2 * CH :].astype(BF16)


def low_half():
    return iota((256, 128), 1) < HD


def only(half, values):
    low = low_half()
    keep = low if half == 0 else jnp.logical_not(low)
    return jnp.where(keep, values, jnp.zeros_like(values))


def softmax(query, keys):
    expo = jnp.exp(nt(query, keys) * 0.125)
    return expo * (1.0 / jnp.sum(expo, axis=-1, keepdims=True))


def attend_back(qkn, v, gmix, pair, recalled):
    at = slice(pair * 128, pair * 128 + 128)
    q2, k2, v2 = qkn[:, at], qkn[:, CH + pair * 128 : CH + pair * 128 + 128], v[:, at]
    g2 = gmix[:, at]
    g2f = g2.astype(F32)
    low = low_half()
    mix, gq, gk, gv = [], [], [], []
    for h in range(2):
        if recalled is None:
            weights = softmax(only(h, q2), k2)
            rounded = weights.astype(BF16)
            mix.append(nn(rounded, v2))
            inner = jnp.sum(only(h, g2f * mix[h]), axis=-1, keepdims=True)
        else:
            rounded = recalled[0][2 * pair + h]
            weights = rounded.astype(F32)
            inner = jnp.sum(only(h, g2f * recalled[1][:, at].astype(F32)), axis=-1, keepdims=True)
        gweights = nt(only(h, g2), v2)
        gscores = (weights * (gweights - inner) * 0.125).astype(BF16)
        gv.append(tn(rounded, g2))
        gq.append(nn(gscores, k2))
        gk.append(tn(gscores, q2))
    return (
        jnp.where(low, mix[0], mix[1]) if recalled is None else None,
        jnp.where(low, gq[0], gq[1]),
        jnp.where(low, gk[0], gk[1]),
        jnp.where(low, gv[0], gv[1]),
    )


def forward_kernel(take, give):
    x = take(0)[...].astype(F32)
    normed, scale, qkn, v = project(x, take(1))
    give(1, normed)
    give(2, scale)
    give(3, qkn)
    give(4, v)
    weights, mixed = [], []
    for pair in range(HEADS // 2):
        at = slice(pair * 128, pair * 128 + 128)
        q2, k2, v2 = qkn[:, at], qkn[:, CH + pair * 128 : CH + pair * 128 + 128], v[:, at]
        parts = []
        for h in range(2):
            rounded = softmax(only(h, q2), k2).astype(BF16)
            weights.append(rounded)
            parts.append(nn(rounded, v2))
        mixed.append(jnp.where(low_half(), parts[0], parts[1]).astype(BF16))
    give(5, jnp.stack(weights))
    mixed = jnp.concatenate(mixed, axis=1)
    give(6, mixed)
    y = (x + nn(mixed, take(2)[...])).astype(BF16)
    give(0, swap_order(y).reshape(256, 2, 256))


def backward_tail(
    x, g, take_wq, scale, qkn, v, gmix, recalled, give_terms
):
    gqs, gks, gvs, mixed = [], [], [], []
    for pair in range(HEADS // 2):
        mix, gq, gk, gv = attend_back(qkn, v, gmix, pair, recalled)
        if recalled is None:
            mixed.append(mix.astype(BF16))
        gqs.append(gq.astype(BF16))
        gks.append(gk.astype(BF16))
        gvs.append(gv.astype(BF16))
    gqk = jnp.concatenate(gqs + gks, axis=1).astype(F32)
    yn = qkn.astype(F32)
    gqk = scale * (gqk - yn * head_means(yn * gqk))
    gqk = gqk.astype(BF16)
    gqkv = [gqk[:, :CH], gqk[:, CH:], jnp.concatenate(gvs, axis=1)]
    give_terms(mixed, gqkv)
    gnormed = nt(jnp.concatenate(gqkv, axis=1), take_wq()[...]).astype(BF16).astype(F32)
    r = inv_rms(x)
    xn = x * r
    gx = g + r * (gnormed - xn * jnp.mean(xn * gnormed, axis=-1, keepdims=True))
    return gx.astype(BF16), mixed


def both_kernel(at_ref, take, give):
    x = take(0)[...].astype(F32).reshape(256, CH)
    normed, scale, qkn, v = project(x, take(1))
    g = unpack_rows([take(3 + k) for k in range(4)], functools.partial(row_away, at_ref), False)
    give(5, normed, (slice(None), slice(0, CH)))
    give(6, g, (slice(None), slice(3 * CH, 4 * CH)))
    wo = take(2)[...]

    def give_terms(mixed, gqkv):
        give(5, jnp.concatenate(mixed, axis=1), (slice(None), slice(CH, 2 * CH)))
        give(5)
        for k, part in enumerate(gqkv):
            give(6, part, (slice(None), slice(k * CH, k * CH + CH)))
        give(6)

    gx, mixed = backward_tail(
        x,
        g.astype(F32),
        lambda: take(1),
        scale,
        qkn,
        v,
        nt(g, wo).astype(BF16),
        None,
        give_terms,
    )
    give(0, gx.reshape(256, 2, 256))
    y = (x + nn(jnp.concatenate(mixed, axis=1), wo)).astype(BF16)
    for k, part in enumerate(pack_rows(y, functools.partial(turned_device, at_ref), True)):
        give(1 + k, part)


def back_kernel(at_ref, take, give):
    g = swap_order(take(0)[...].astype(F32).reshape(256, CH).astype(BF16))
    give(7, g)
    wo = take(1)[...]
    gmix = nt(g, wo).astype(BF16)
    v, recalled, qkn = take(2)[...], (take(3), take(4)), take(5)[...]
    scale, x = take(6)[...], take(7)[...].astype(F32)
    gx, _ = backward_tail(
        x,
        g.astype(F32),
        lambda: take(8),
        scale,
        qkn,
        v,
        gmix,
        recalled,
        lambda _, gqkv: [give(4 + k, part) for k, part in enumerate(gqkv)],
    )
    for k, part in enumerate(pack_rows(gx, functools.partial(col_device, at_ref), True)):
        give(k, part)


def finish_kernel(sums_ref, *refs):
    totals = jnp.sum(sums_ref[...].astype(F32), axis=0)
    for k in range(2):
        refs[2 * k][...] = totals[k, :, :96]
        refs[2 * k + 1][...] = totals[k, :, 96:]


def weights_kernel(at_ref, take, give):
    core = at_ref[2]
    col = iota((CH, 256), 1)
    order = (iota((CH, 256), 0) == (col >> 5) * 64 + core * 32 + (col & 31)).astype(BF16)
    row, col = iota((CH, CH), 0), iota((CH, CH), 1)
    lane = col & 127
    near = (row == (col >> 7) * 96 + lane) & (lane < 96)
    far = (row == 384 + (col >> 7) * 32 + lane - 96) & (lane >= 96)
    spread = (near | far).astype(BF16)
    normed, mixed = (
        jnp.concatenate([nn(take(2 * i + k)[...], order).astype(BF16) for k in (0, 1)], axis=0)
        for i in range(2)
    )
    ggs = [[take(2 * i + k) for i in range(2, 6)] for k in (0, 1)]
    for group in range(4):
        blocks = [divmod(3 * group + k, 4) for k in range(3)]
        gqkv, g = [], []
        for gg in ggs:
            part = [gg[i][:, k * 128 : k * 128 + 128] for i, k in blocks]
            gqkv.append(jnp.concatenate(part, axis=1))
            g.append(gg[3][:, group * 128 : group * 128 + 128])
        gqkv, g = jnp.concatenate(gqkv, axis=0), jnp.concatenate(g, axis=0)
        total = jnp.concatenate([tn(normed, gqkv), tn(mixed, g)], axis=1).astype(BF16)
        total = nn(total, spread).astype(BF16)
        for xz in range(8):
            for y in range(4):
                piece = total[xz * 32 : xz * 32 + 32, y * 128 : y * 128 + 128]
                give(0, piece, ((xz >> 1) * 4 + y, group * 2 + (xz & 1)))
        give(0, part=(slice(None), pl.ds(group * 2, 2)))


WHOLE = pl.BlockSpec()
ANY = pl.BlockSpec(memory_space=pl.ANY)
SMEM = pl.BlockSpec(memory_space=pltpu.SMEM)
MIB = 2**20
ROOM = 64


def shape(*dims, dtype=BF16):
    return jax.ShapeDtypeStruct(dims, dtype)


def costs(args, outs, flops):
    nbytes = 1 if flops == 1 else sum(a.size * a.dtype.itemsize for a in (*args, *outs))
    return pl.CostEstimate(flops=flops, bytes_accessed=nbytes, transcendentals=0)


def call(kernel, outs, specs, args, room=8):
    return pl.pallas_call(
        kernel,
        out_shape=outs,
        in_specs=specs,
        out_specs=[WHOLE] * len(outs),
        compiler_params=pltpu.CompilerParams(vmem_limit_bytes=room * MIB),
        cost_estimate=costs(args, outs, 1),
    )(*args)


def stream(kernel, outs, args, flops=1, at=None, room=ROOM):
    first, n, m = int(at is not None), len(args), len(outs)

    def body(*refs):
        ins, results = refs[first : first + n], refs[first + n : first + n + m]
        scratch = refs[first + n + m :]
        made, here = scratch[:m], scratch[m : m + n]
        in_sem, out_sem = refs[-2:]
        arrive = {i: pltpu.make_async_copy(ins[i], here[i], in_sem.at[i]) for i in range(n)}
        leave = []
        for copy in arrive.values():
            copy.start()

        def take(i):
            if i in arrive:
                arrive.pop(i).wait()
            return here[i]

        def give(j, value=None, place=..., part=...):
            if value is not None:
                made[j][place] = value
            if value is None or place is ...:
                sem = out_sem.at[len(leave)]
                leave.append(pltpu.make_async_copy(made[j].at[part], results[j].at[part], sem))
                leave[-1].start()

        kernel(*refs[:first], take, give)
        for copy in leave:
            copy.wait()

    buffers = [pltpu.VMEM(a.shape, a.dtype) for a in (*outs, *args)]
    sems = [pltpu.SemaphoreType.DMA((n,)), pltpu.SemaphoreType.DMA((m + 4,))]
    return pl.pallas_call(
        body,
        out_shape=outs,
        in_specs=[SMEM] * first + [ANY] * n,
        out_specs=[ANY] * m,
        scratch_shapes=buffers + sems,
        compiler_params=pltpu.CompilerParams(vmem_limit_bytes=room * MIB),
        cost_estimate=costs(args, outs, flops),
    )(*([at] if first else []), *args)


def weight_terms(at, factors, swapped=()):
    others = [*swapped, *map(swap_cores, factors[len(swapped) :])]
    factors = [half for both in zip(factors, others) for half in both]

    def kernel(at_ref, take, give):
        def part(i):
            k, c = divmod(i, 2)
            first, which = (0, k) if k < 2 else (2, k - 2)
            return take(first + c).at[:, which * CH : which * CH + CH]

        weights_kernel(at_ref, take if len(factors) == 12 else part, give)

    return stream(kernel, [shape(16, 8, 32, 128)], factors, at=at)[0]


def swap_cores(values):
    return lax.ppermute(values, "core", [(0, 1), (1, 0)])


def a2a(values, axes):
    return lax.all_to_all(values, axes, split_axis=0, concat_axis=0, tiled=True)


def around(parts, axis):
    n = len(parts)
    return [parts[0]] + [
        lax.ppermute(parts[k], axis, [(i, (i + k) % n) for i in range(n)]) for k in range(1, n)
    ]


def bit_hop(parts, near=None):
    def move(zc):
        return lax.ppermute(parts[zc], ("zh", "core"), [(i, i ^ zc) for i in range(4)])

    return [parts[0], move(1) if near is None else near, move(2), move(3)]


def regroup(parts):
    return call(regroup_kernel, [shape(64, CH)] * len(parts), [WHOLE] * len(parts), parts)


def together(*values):
    return lax.optimization_barrier(values)


def line_sum(values):
    return jnp.sum(values.astype(F32), axis=0).astype(BF16)


def on_device(latent, grad_latent, w_qkv_row, w_out_row, w_qkv_col, w_out_col):
    at = [lax.axis_index(name) for name in ("x", "zh", "core", "zl", "y")]
    at = jnp.stack(at).astype(jnp.int32)
    cells, sent = shape(256, CH), shape(256, 2, 256)
    grad_latent = grad_latent.reshape(256, CH)
    g_col = call(pack_kernel, [shape(64, CH)] * 4, [SMEM, WHOLE], (at, grad_latent))
    g_col = bit_hop(g_col)
    x_row = a2a(latent, COL).reshape(256, CH)
    mid_row, normed_r, scale_r, qkn_r, v_r, weights_r, mixed_r = stream(
        forward_kernel,
        [
            sent,
            cells,
            shape(256, 2 * CH, dtype=F32),
            shape(256, 2 * CH),
            cells,
            shape(HEADS, 256, 256),
            cells,
        ],
        (x_row, w_qkv_row, w_out_row),
        10**9,
        room=63,
    )
    mid_row, g_col = together(mid_row, g_col)
    g_col = around(regroup(g_col), "x")
    x_col = a2a(mid_row, ROW + COL)
    x_col, *swapped = together(x_col, swap_cores(normed_r), swap_cores(mixed_r))
    gx_col, *parts = stream(
        both_kernel,
        [sent] + [shape(64, CH)] * 4 + [shape(256, 2 * CH), shape(256, 4 * CH)],
        (x_col, w_qkv_col, w_out_col, *g_col),
        3 * 10**9,
        at,
    )
    y_col, factors_c = parts[:4], parts[4:]
    g_row = a2a(gx_col, ROW + COL)
    terms = weight_terms(at, factors_c)
    y_col = around(y_col, "x")
    g_row, terms, *y_col = together(g_row, terms, *y_col)
    parts = stream(
        back_kernel,
        [shape(64, CH)] * 4 + [cells] * 4,
        (g_row, w_out_row, v_r, weights_r, mixed_r, qkn_r, scale_r, x_row, w_qkv_row),
        2 * 10**9,
        at,
    )
    sums_c = a2a(terms, ("x", "y"))
    gx_row = parts[:4]
    terms = weight_terms(at, [normed_r, mixed_r, *parts[4:]], swapped)
    sums_c, terms = together(sums_c, terms)
    sums_r = a2a(terms, ("x", "y"))
    y_col = regroup(y_col)
    near, *gx_row = together(swap_cores(y_col[1]), *gx_row)
    y_col = bit_hop(y_col, near)
    gx_row = around(gx_row, "zl")
    sums = jnp.stack([line_sum(sums_r), line_sum(sums_c)], axis=1)
    sums, *parts = together(sums, *y_col, *gx_row)
    sums = a2a(sums, ("zl", "zh"))
    parts = parts[:4] + around(regroup(parts[4:]), "y")
    final, grad_input = call(unpack_kernel, [cells] * 2, [SMEM] + [WHOLE] * 8, (at, *parts))
    final, grad_input = final.reshape(16, 16, CH), grad_input.reshape(16, 16, CH)
    gq, go = shape(32, 96, dtype=F32), shape(32, 32, dtype=F32)
    grads = call(finish_kernel, [gq, go] * 2, [WHOLE], (sums,))
    return (final, grad_input, *grads)


def solution(mesh):
    fine = Mesh(mesh.devices.reshape(4, 2, 2, 4, 4), ("x", "zh", "core", "zl", "y"))
    in_specs = (P(ROW, COL, None), P(ROW, COL, None), P(), P(), P(), P())
    out_specs = (
        P(ROW, COL, None),
        P(ROW, COL, None),
        P(ROW, COL),
        P(ROW, COL),
        P(ROW, COL),
        P(ROW, COL),
    )
    return jax.shard_map(
        on_device, mesh=fine, in_specs=in_specs, out_specs=out_specs, check_vma=False
    )
```

```python
import functools

import jax
import jax.numpy as jnp
from jax import lax
from jax.experimental import pallas as pl
from jax.experimental.pallas import tpu as pltpu
from jax.sharding import Mesh
from jax.sharding import PartitionSpec as P

HEADS = 8
HD = 64
CH = 512
EPS = 1e-06
F32 = jnp.float32
BF16 = jnp.bfloat16

ROW = ("x", "zh", "core")
COL = ("zl", "y")


def nn(a, b):
    return jnp.dot(a, b, preferred_element_type=F32)


def nt(a, b):
    return lax.dot_general(a, b, (((1,), (1,)), ((), ())), preferred_element_type=F32)


def tn(a, b):
    return lax.dot_general(a, b, (((0,), (0,)), ((), ())), preferred_element_type=F32)


def iota(shape, dim):
    return lax.broadcasted_iota(jnp.int32, shape, dim)


def head_means(values):
    low, parts = low_half(), []
    for at in range(0, 2 * CH, 128):
        pair = values[:, at : at + 128]
        first = jnp.sum(jnp.where(low, pair, 0.0), axis=-1, keepdims=True)
        second = jnp.sum(jnp.where(low, 0.0, pair), axis=-1, keepdims=True)
        parts.append(jnp.where(low, first, second))
    return jnp.concatenate(parts, axis=1) * (1.0 / HD)


def inv_rms(x):
    return lax.rsqrt(jnp.mean(x * x, axis=-1, keepdims=True) + EPS)


def swap_order(values):
    rows = iota((256, 256), 0)
    cols = iota((256, 256), 1)
    swap = ((rows & 15) * 16 + (rows >> 4) == cols).astype(BF16)
    return nn(swap, values).astype(BF16)


def rows_from(source, values):
    return nn((iota((256, 256), 1) == source).astype(BF16), values).astype(BF16)


def pack_rows(values, device, inner_first):
    row = iota((256, 256), 0)
    to, cell = device(row >> 6, (row >> 4) & 3), row & 15
    packed = rows_from(to * 16 + cell if inner_first else cell * 16 + to, values)
    return [packed[k * 64 : k * 64 + 64] for k in range(4)]


def unpack_rows(refs, away, cell_first):
    row = iota((256, 256), 0)
    device, cell = (row & 15, row >> 4) if cell_first else (row >> 4, row & 15)
    one, two = away(device)
    values = jnp.concatenate([ref[...] for ref in refs], axis=0)
    return rows_from(two * 64 + one * 16 + cell, values)


def row_device(at_ref, one, two):
    return ((at_ref[0] + two) & 3) * 4 + (one ^ (at_ref[1] * 2 + at_ref[2]))


def row_away(at_ref, device):
    return (device & 3) ^ (at_ref[1] * 2 + at_ref[2]), (at_ref[0] - (device >> 2)) & 3


def turned_device(at_ref, one, two):
    return row_device(at_ref, two, one)


def turned_away(at_ref, device):
    return row_away(at_ref, device)[::-1]


def col_device(at_ref, one, two):
    return ((at_ref[3] + one) & 3) * 4 + ((at_ref[4] + two) & 3)


def col_away(at_ref, device):
    return (at_ref[3] - (device >> 2)) & 3, (at_ref[4] - (device & 3)) & 3


def pack_kernel(at_ref, g_ref, *refs):
    parts = pack_rows(g_ref[...], functools.partial(row_device, at_ref), False)
    for ref, part in zip(refs, parts):
        ref[...] = part


def unpack_kernel(at_ref, *refs):
    refs[8][...] = unpack_rows(refs[:4], functools.partial(turned_away, at_ref), True)
    refs[9][...] = unpack_rows(refs[4:8], functools.partial(col_away, at_ref), False)


def regroup_kernel(*refs):
    n = len(refs) // 2
    for first in range(0, n, 4):
        for two in range(4):
            for one in range(4):
                part = refs[first + one][two * 16 : two * 16 + 16]
                refs[n + first + two][one * 16 : one * 16 + 16] = part


def project(x, w_qkv):
    normed = (x * inv_rms(x)).astype(BF16)
    qkv = nn(normed, w_qkv[...])
    qk = qkv[:, : 2 * CH]
    scale = lax.rsqrt(head_means(qk * qk) + EPS)
    qkn = (qk * scale).astype(BF16)
    return normed, scale, qkn, qkv[:, 2 * CH :].astype(BF16)


def low_half():
    return iota((256, 128), 1) < HD


def only(half, values):
    low = low_half()
    keep = low if half == 0 else jnp.logical_not(low)
    return jnp.where(keep, values, jnp.zeros_like(values))


def softmax(query, keys):
    expo = jnp.exp(nt(query, keys) * 0.125)
    return expo * (1.0 / jnp.sum(expo, axis=-1, keepdims=True))


def attend_back(qkn, v, gmix, pair, recalled):
    at = slice(pair * 128, pair * 128 + 128)
    q2, k2, v2 = qkn[:, at], qkn[:, CH + pair * 128 : CH + pair * 128 + 128], v[:, at]
    g2 = gmix[:, at]
    g2f = g2.astype(F32)
    low = low_half()
    mix, gq, gk, gv = [], [], [], []
    for h in range(2):
        if recalled is None:
            weights = softmax(only(h, q2), k2)
            rounded = weights.astype(BF16)
            mix.append(nn(rounded, v2))
            inner = jnp.sum(only(h, g2f * mix[h]), axis=-1, keepdims=True)
        else:
            rounded = recalled[0][2 * pair + h]
            weights = rounded.astype(F32)
            inner = jnp.sum(only(h, g2f * recalled[1][:, at].astype(F32)), axis=-1, keepdims=True)
        gweights = nt(only(h, g2), v2)
        gscores = (weights * (gweights - inner) * 0.125).astype(BF16)
        gv.append(tn(rounded, g2))
        gq.append(nn(gscores, k2))
        gk.append(tn(gscores, q2))
    return (
        jnp.where(low, mix[0], mix[1]) if recalled is None else None,
        jnp.where(low, gq[0], gq[1]),
        jnp.where(low, gk[0], gk[1]),
        jnp.where(low, gv[0], gv[1]),
    )


def forward_kernel(take, give):
    x = take(0)[...].astype(F32)
    normed, scale, qkn, v = project(x, take(1))
    give(1, normed)
    give(2, scale)
    give(3, qkn)
    give(4, v)
    weights, mixed = [], []
    for pair in range(HEADS // 2):
        at = slice(pair * 128, pair * 128 + 128)
        q2, k2, v2 = qkn[:, at], qkn[:, CH + pair * 128 : CH + pair * 128 + 128], v[:, at]
        parts = []
        for h in range(2):
            rounded = softmax(only(h, q2), k2).astype(BF16)
            weights.append(rounded)
            parts.append(nn(rounded, v2))
        mixed.append(jnp.where(low_half(), parts[0], parts[1]).astype(BF16))
    give(5, jnp.stack(weights))
    mixed = jnp.concatenate(mixed, axis=1)
    give(6, mixed)
    y = (x + nn(mixed, take(2)[...])).astype(BF16)
    give(0, swap_order(y).reshape(256, 2, 256))


def backward_tail(
    x, g, take_wq, scale, qkn, v, gmix, recalled, give_terms
):
    gqs, gks, gvs, mixed = [], [], [], []
    for pair in range(HEADS // 2):
        mix, gq, gk, gv = attend_back(qkn, v, gmix, pair, recalled)
        if recalled is None:
            mixed.append(mix.astype(BF16))
        gqs.append(gq.astype(BF16))
        gks.append(gk.astype(BF16))
        gvs.append(gv.astype(BF16))
    gqk = jnp.concatenate(gqs + gks, axis=1).astype(F32)
    yn = qkn.astype(F32)
    gqk = scale * (gqk - yn * head_means(yn * gqk))
    gqk = gqk.astype(BF16)
    gqkv = [gqk[:, :CH], gqk[:, CH:], jnp.concatenate(gvs, axis=1)]
    give_terms(mixed, gqkv)
    gnormed = nt(jnp.concatenate(gqkv, axis=1), take_wq()[...]).astype(BF16).astype(F32)
    r = inv_rms(x)
    xn = x * r
    gx = g + r * (gnormed - xn * jnp.mean(xn * gnormed, axis=-1, keepdims=True))
    return gx.astype(BF16), mixed


def both_kernel(at_ref, take, give):
    x = take(0)[...].astype(F32).reshape(256, CH)
    normed, scale, qkn, v = project(x, take(1))
    g = unpack_rows([take(3 + k) for k in range(4)], functools.partial(row_away, at_ref), False)
    give(5, normed, (slice(None), slice(0, CH)))
    give(6, g, (slice(None), slice(3 * CH, 4 * CH)))
    wo = take(2)[...]

    def give_terms(mixed, gqkv):
        give(5, jnp.concatenate(mixed, axis=1), (slice(None), slice(CH, 2 * CH)))
        give(5)
        for k, part in enumerate(gqkv):
            give(6, part, (slice(None), slice(k * CH, k * CH + CH)))
        give(6)

    gx, mixed = backward_tail(
        x,
        g.astype(F32),
        lambda: take(1),
        scale,
        qkn,
        v,
        nt(g, wo).astype(BF16),
        None,
        give_terms,
    )
    give(0, gx.reshape(256, 2, 256))
    y = (x + nn(jnp.concatenate(mixed, axis=1), wo)).astype(BF16)
    for k, part in enumerate(pack_rows(y, functools.partial(turned_device, at_ref), True)):
        give(1 + k, part)


def back_kernel(at_ref, take, give):
    g = swap_order(take(0)[...].astype(F32).reshape(256, CH).astype(BF16))
    give(7, g)
    wo = take(1)[...]
    gmix = nt(g, wo).astype(BF16)
    v, recalled, qkn = take(2)[...], (take(3), take(4)), take(5)[...]
    scale, x = take(6)[...], take(7)[...].astype(F32)
    gx, _ = backward_tail(
        x,
        g.astype(F32),
        lambda: take(8),
        scale,
        qkn,
        v,
        gmix,
        recalled,
        lambda _, gqkv: [give(4 + k, part) for k, part in enumerate(gqkv)],
    )
    for k, part in enumerate(pack_rows(gx, functools.partial(col_device, at_ref), True)):
        give(k, part)


def finish_kernel(sums_ref, *refs):
    totals = jnp.sum(sums_ref[...].astype(F32), axis=0)
    for k in range(2):
        refs[2 * k][...] = totals[k, :, :96]
        refs[2 * k + 1][...] = totals[k, :, 96:]


def weights_kernel(at_ref, take, give):
    core = at_ref[2]
    col = iota((CH, 256), 1)
    order = (iota((CH, 256), 0) == (col >> 5) * 64 + core * 32 + (col & 31)).astype(BF16)
    row, col = iota((CH, CH), 0), iota((CH, CH), 1)
    lane = col & 127
    near = (row == (col >> 7) * 96 + lane) & (lane < 96)
    far = (row == 384 + (col >> 7) * 32 + lane - 96) & (lane >= 96)
    spread = (near | far).astype(BF16)
    normed, mixed = (
        jnp.concatenate([nn(take(2 * i + k)[...], order).astype(BF16) for k in (0, 1)], axis=0)
        for i in range(2)
    )
    ggs = [[take(2 * i + k) for i in range(2, 6)] for k in (0, 1)]
    for group in range(4):
        blocks = [divmod(3 * group + k, 4) for k in range(3)]
        gqkv, g = [], []
        for gg in ggs:
            part = [gg[i][:, k * 128 : k * 128 + 128] for i, k in blocks]
            gqkv.append(jnp.concatenate(part, axis=1))
            g.append(gg[3][:, group * 128 : group * 128 + 128])
        gqkv, g = jnp.concatenate(gqkv, axis=0), jnp.concatenate(g, axis=0)
        total = jnp.concatenate([tn(normed, gqkv), tn(mixed, g)], axis=1).astype(BF16)
        total = nn(total, spread).astype(BF16)
        for xz in range(8):
            for y in range(4):
                piece = total[xz * 32 : xz * 32 + 32, y * 128 : y * 128 + 128]
                give(0, piece, ((xz >> 1) * 4 + y, group * 2 + (xz & 1)))
        give(0, part=(slice(None), pl.ds(group * 2, 2)))


WHOLE = pl.BlockSpec()
ANY = pl.BlockSpec(memory_space=pl.ANY)
SMEM = pl.BlockSpec(memory_space=pltpu.SMEM)
MIB = 2**20
ROOM = 64


def shape(*dims, dtype=BF16):
    return jax.ShapeDtypeStruct(dims, dtype)


def costs(args, outs, flops):
    nbytes = 1 if flops == 1 else sum(a.size * a.dtype.itemsize for a in (*args, *outs))
    return pl.CostEstimate(flops=flops, bytes_accessed=nbytes, transcendentals=0)


def call(kernel, outs, specs, args, room=8):
    return pl.pallas_call(
        kernel,
        out_shape=outs,
        in_specs=specs,
        out_specs=[WHOLE] * len(outs),
        compiler_params=pltpu.CompilerParams(vmem_limit_bytes=room * MIB),
        cost_estimate=costs(args, outs, 1),
    )(*args)


def stream(kernel, outs, args, flops=1, at=None, room=ROOM):
    first, n, m = int(at is not None), len(args), len(outs)

    def body(*refs):
        ins, results = refs[first : first + n], refs[first + n : first + n + m]
        scratch = refs[first + n + m :]
        made, here = scratch[:m], scratch[m : m + n]
        in_sem, out_sem = refs[-2:]
        arrive = {i: pltpu.make_async_copy(ins[i], here[i], in_sem.at[i]) for i in range(n)}
        leave = []
        for copy in arrive.values():
            copy.start()

        def take(i):
            if i in arrive:
                arrive.pop(i).wait()
            return here[i]

        def give(j, value=None, place=..., part=...):
            if value is not None:
                made[j][place] = value
            if value is None or place is ...:
                sem = out_sem.at[len(leave)]
                leave.append(pltpu.make_async_copy(made[j].at[part], results[j].at[part], sem))
                leave[-1].start()

        kernel(*refs[:first], take, give)
        for copy in leave:
            copy.wait()

    buffers = [pltpu.VMEM(a.shape, a.dtype) for a in (*outs, *args)]
    sems = [pltpu.SemaphoreType.DMA((n,)), pltpu.SemaphoreType.DMA((m + 4,))]
    return pl.pallas_call(
        body,
        out_shape=outs,
        in_specs=[SMEM] * first + [ANY] * n,
        out_specs=[ANY] * m,
        scratch_shapes=buffers + sems,
        compiler_params=pltpu.CompilerParams(vmem_limit_bytes=room * MIB),
        cost_estimate=costs(args, outs, flops),
    )(*([at] if first else []), *args)


def weight_terms(at, factors, swapped=()):
    others = [*swapped, *map(swap_cores, factors[len(swapped) :])]
    factors = [half for both in zip(factors, others) for half in both]

    def kernel(at_ref, take, give):
        def part(i):
            k, c = divmod(i, 2)
            first, which = (0, k) if k < 2 else (2, k - 2)
            return take(first + c).at[:, which * CH : which * CH + CH]

        weights_kernel(at_ref, take if len(factors) == 12 else part, give)

    return stream(kernel, [shape(16, 8, 32, 128)], factors, at=at)[0]


def swap_cores(values):
    return lax.ppermute(values, "core", [(0, 1), (1, 0)])


def a2a(values, axes):
    return lax.all_to_all(values, axes, split_axis=0, concat_axis=0, tiled=True)


def around(parts, axis):
    n = len(parts)
    return [parts[0]] + [
        lax.ppermute(parts[k], axis, [(i, (i + k) % n) for i in range(n)]) for k in range(1, n)
    ]


def bit_hop(parts, near=None):
    def move(zc):
        return lax.ppermute(parts[zc], ("zh", "core"), [(i, i ^ zc) for i in range(4)])

    return [parts[0], move(1) if near is None else near, move(2), move(3)]


def regroup(parts):
    return call(regroup_kernel, [shape(64, CH)] * len(parts), [WHOLE] * len(parts), parts)


def together(*values):
    return lax.optimization_barrier(values)


def line_sum(values):
    return jnp.sum(values.astype(F32), axis=0).astype(BF16)


def on_device(latent, grad_latent, w_qkv_row, w_out_row, w_qkv_col, w_out_col):
    at = [lax.axis_index(name) for name in ("x", "zh", "core", "zl", "y")]
    at = jnp.stack(at).astype(jnp.int32)
    cells, sent = shape(256, CH), shape(256, 2, 256)
    grad_latent = grad_latent.reshape(256, CH)
    g_col = call(pack_kernel, [shape(64, CH)] * 4, [SMEM, WHOLE], (at, grad_latent))
    g_col = bit_hop(g_col)
    x_row = a2a(latent, COL).reshape(256, CH)
    mid_row, normed_r, scale_r, qkn_r, v_r, weights_r, mixed_r = stream(
        forward_kernel,
        [
            sent,
            cells,
            shape(256, 2 * CH, dtype=F32),
            shape(256, 2 * CH),
            cells,
            shape(HEADS, 256, 256),
            cells,
        ],
        (x_row, w_qkv_row, w_out_row),
        10**9,
        room=63,
    )
    mid_row, g_col = together(mid_row, g_col)
    g_col = around(regroup(g_col), "x")
    x_col = a2a(mid_row, ROW + COL)
    *g_col, normed_2, mixed_2 = together(*g_col, swap_cores(normed_r), swap_cores(mixed_r))
    gx_col, *parts = stream(
        both_kernel,
        [sent] + [shape(64, CH)] * 4 + [shape(256, 2 * CH), shape(256, 4 * CH)],
        (x_col, w_qkv_col, w_out_col, *g_col),
        3 * 10**9,
        at,
    )
    y_col, factors_c = parts[:4], parts[4:]
    g_row = a2a(gx_col, ROW + COL)
    terms = weight_terms(at, factors_c)
    y_col = around(y_col, "x")
    g_row, terms, *y_col = together(g_row, terms, *y_col)
    parts = stream(
        back_kernel,
        [shape(64, CH)] * 4 + [cells] * 4,
        (g_row, w_out_row, v_r, weights_r, mixed_r, qkn_r, scale_r, x_row, w_qkv_row),
        2 * 10**9,
        at,
    )
    sums_c = a2a(terms, ("x", "y"))
    gx_row = parts[:4]
    terms = weight_terms(at, [normed_r, mixed_r, *parts[4:]], (normed_2, mixed_2))
    sums_c, terms = together(sums_c, terms)
    sums_r = a2a(terms, ("x", "y"))
    y_col = regroup(y_col)
    near, *gx_row = together(swap_cores(y_col[1]), *gx_row)
    y_col = bit_hop(y_col, near)
    gx_row = around(gx_row, "zl")
    sums = jnp.stack([line_sum(sums_r), line_sum(sums_c)], axis=1)
    sums, *parts = together(sums, *y_col, *gx_row)
    sums = a2a(sums, ("zl", "zh"))
    parts = parts[:4] + around(regroup(parts[4:]), "y")
    final, grad_input = call(unpack_kernel, [cells] * 2, [SMEM] + [WHOLE] * 8, (at, *parts))
    final, grad_input = final.reshape(16, 16, CH), grad_input.reshape(16, 16, CH)
    gq, go = shape(32, 96, dtype=F32), shape(32, 32, dtype=F32)
    grads = call(finish_kernel, [gq, go] * 2, [WHOLE], (sums,))
    return (final, grad_input, *grads)


def solution(mesh):
    fine = Mesh(mesh.devices.reshape(4, 2, 2, 4, 4), ("x", "zh", "core", "zl", "y"))
    in_specs = (P(ROW, COL, None), P(ROW, COL, None), P(), P(), P(), P())
    out_specs = (
        P(ROW, COL, None),
        P(ROW, COL, None),
        P(ROW, COL),
        P(ROW, COL),
        P(ROW, COL),
        P(ROW, COL),
    )
    return jax.shard_map(
        on_device, mesh=fine, in_specs=in_specs, out_specs=out_specs, check_vma=False
    )
```
